32 devices in a mesh: dp: 2 (over x), ctx: 16 (over z, y, core).
Axes of the slice: x: 2, y: 2, z: 4, core: 2. Of those that a mesh axis runs over, the one named last changes fastest.
Arguments:
- level_input: bfloat16 [2, 16384, 256], P('dp', 'ctx'), may hold values from -6 to 6
- saved_forward: bfloat16 [3, 2, 16384, 256], P(None, 'dp', 'ctx'), may hold values from -6 to 6
- saved_reverse: bfloat16 [3, 2, 16384, 256], P(None, 'dp', 'ctx'), may hold values from -6 to 6
- filters: float32 [2, 2, 2, 256], replicated, may hold values from -2.5 to 2.5
- mixing: float32 [2, 5, 256], replicated, may hold values from -3 to 3
- cotangent: bfloat16 [2, 16384, 256], P('dp', 'ctx'), may hold values from -33 to 33
Outputs:
- grad_input: bfloat16 [2, 16384, 256], P('dp', 'ctx')
- grad_filters: float32 [2, 2, 2, 256], replicated
- grad_mixing: float32 [2, 5, 256], replicated
The draws below stay inside these ranges and needn't reach their ends.
All inputs are finite; a program needn't handle non-finite values.
Results may differ from the reference program's by a relative error of at most 0.0065.
Values may be sent and summed in bfloat16 or wider, within the bound.
A program may use at most 64 MiB of HBM per device.

```python
import math
import jax
import jax.numpy as jnp
from jax import lax

C = 256
LEVELS = 4
BASE = 128
SEQS = 2
LENGTH = 16384


def draw_cotangent(key, part):
    key = jax.random.fold_in(key, 7)
    first = jax.random.fold_in(key, 0)
    shape = (SEQS, LENGTH, C)
    where = jnp.arange(LENGTH, dtype=jnp.float32) / (LENGTH - 1)
    ramp = jnp.exp(math.log(3.0) * where)[None, :, None]
    values = jnp.clip(jax.random.normal(first, shape, jnp.float32), -5.0, 5.0)
    return (values * ramp).astype(jnp.bfloat16)


def block_scale(stream_key, shape, cuts, least, high):
    def one(position, blocks):
        draws = jax.random.uniform(jax.random.fold_in(jax.random.fold_in(stream_key, 6), position), (blocks,), jnp.float32, least / len(cuts), high / len(cuts))
        return jnp.repeat(jnp.exp(draws), shape[position] // blocks).reshape((-1,) + (1,) * (len(shape) - position - 1))

    loudness = one(*cuts[0])
    for cut in cuts[1:]:
        loudness = loudness * one(*cut)
    return loudness


def centred(stream_key, dims, width, most, shards=(), held_as=jnp.bfloat16):
    values = width * jax.random.normal(stream_key, dims, jnp.float32)
    if shards:
        values = values * block_scale(stream_key, dims, shards, -0.22, 0.18)
    return jnp.clip(values, -most, most).astype(held_as)


def setup_inputs(seed: int = 0) -> dict:
    seeds = jax.random.split(jax.random.key(seed), 7)
    level_input = centred(seeds[0], (SEQS, LENGTH, C), 1.0, 6.0, ((0, 2), (1, 16)))
    saved_forward = centred(seeds[1], (LEVELS - 1, SEQS, LENGTH, C), 1.0, 6.0, ((1, 2), (2, 16)))
    saved_reverse = centred(seeds[2], (LEVELS - 1, SEQS, LENGTH, C), 1.0, 6.0, ((1, 2), (2, 16)))
    filters = centred(seeds[3], (2, 2, 2, C), 0.7, 2.5, (), jnp.float32)
    mixing = centred(seeds[4], (2, LEVELS + 1, C), 0.6, 3.0, (), jnp.float32)
    cotangent = draw_cotangent(jax.random.fold_in(seeds[6], 71), 0)
    return dict(level_input=level_input, saved_forward=saved_forward, saved_reverse=saved_reverse, filters=filters, mixing=mixing, cotangent=cotangent)


def lag(values, dist):
    return jnp.pad(values, ((0, 0), (dist, 0), (0, 0)))[:, :values.shape[1]]

def lead(values, dist):
    return jnp.pad(values, ((0, 0), (0, dist), (0, 0)))[:, dist:]

def branch_backward(inputs, dy, gains, weights, ahead):
    levels = len(inputs)
    grad = weights[levels] * dy
    filt = jnp.zeros((2, 2, C), jnp.float32)
    mixes = [None] * (levels + 1)
    for level in reversed(range(levels)):
        dist = BASE * 2 ** level
        plain = inputs[level].astype(jnp.float32)
        near = lead(plain, dist) if ahead else lag(plain, dist)
        weight = weights[level]
        s_a = lax.optimization_barrier(jnp.sum(grad * near, axis=(0, 1)))
        s_y = lax.optimization_barrier(jnp.sum(dy * near, axis=(0, 1)))
        t_a = lax.optimization_barrier(jnp.sum(grad * plain, axis=(0, 1)))
        t_y = lax.optimization_barrier(jnp.sum(dy * plain, axis=(0, 1)))
        filt = filt + jnp.stack([jnp.stack([s_a, t_a]), jnp.stack([weight * s_y, weight * t_y])])
        mixes[level] = gains[1, 0] * s_y + gains[1, 1] * t_y
        if level == levels - 1:
            mixes[levels] = gains[0, 0] * s_y + gains[0, 1] * t_y
        shifted = gains[0, 0] * grad + gains[1, 0] * (weight * dy)
        back = lag(shifted, dist) if ahead else lead(shifted, dist)
        grad = gains[0, 1] * grad + gains[1, 1] * (weight * dy) + back
    return (grad, filt, jnp.stack(mixes))

def reference(level_input, saved_forward, saved_reverse, filters, mixing, cotangent):
    dy = cotangent.astype(jnp.float32)
    levels = saved_forward.shape[0] + 1
    inputs_fwd = [level_input] + [saved_forward[i] for i in range(levels - 1)]
    inputs_rev = [level_input] + [saved_reverse[i] for i in range(levels - 1)]
    grad_fwd, filt_fwd, mix_fwd = branch_backward(inputs_fwd, dy, filters[0], mixing[0], False)
    grad_rev, filt_rev, mix_rev = branch_backward(inputs_rev, dy, filters[1], mixing[1], True)
    factor = 1.0 / math.sqrt(cotangent.shape[0] * cotangent.shape[1])
    grad_input = (grad_fwd + grad_rev).astype(jnp.bfloat16)
    grad_filters = jnp.stack([filt_fwd, filt_rev]) * factor
    grad_mixing = jnp.stack([mix_fwd, mix_rev]) * factor
    return (grad_input, grad_filters, grad_mixing)
```

```python
import functools
import math

import jax
import jax.numpy as jnp
from jax import lax
from jax.experimental import pallas as pl
from jax.experimental.pallas import tpu as pltpu
from jax.sharding import PartitionSpec as P

BASE = 128
STRIP = 16
LANES = 128
GROUP = 4
MESH = pl.DeviceIdType.MESH
F32 = jnp.float32


def kernel(
    dims,
    cot,
    first,
    fwd,
    rev,
    filt,
    mix,
    out,
    out_filt,
    out_mix,
    dy,
    inputs,
    result,
    sums,
    coef,
    buf_a,
    buf_b,
    load_sem,
    store_sem,
    send_sem,
    recv_sem,
    send_a,
    recv_a,
    send_b,
    recv_b,
):
    n_dp, n_ctx, units, levels, rows, factor = dims
    chunks = BASE // rows
    groups = n_ctx // GROUP
    width = dy.shape[-1]
    top = levels - 1

    dp = lax.axis_index("dp")
    me = lax.axis_index("ctx")
    q = lax.div(me, GROUP)
    r = lax.rem(me, GROUP)
    half = lax.div(r, 2)
    core = lax.rem(r, 2)
    outer = half == core
    sibling = me + 1 - 2 * core
    partner = me + 2 - 4 * half
    has_next = q < groups - 1
    has_prev = q > 0
    lower = half == 0
    z_sends = jnp.logical_or(jnp.logical_and(lower, has_next), jnp.logical_and(half == 1, has_prev))
    z_recvs = jnp.logical_or(jnp.logical_and(lower, has_prev), jnp.logical_and(half == 1, has_next))

    own_load = pltpu.make_async_copy(cot, dy.at[2], load_sem.at[0])
    in_loads = [
        pltpu.make_async_copy(first, inputs.at[0], load_sem.at[1]),
        pltpu.make_async_copy(fwd, inputs.at[pl.ds(1, top)], load_sem.at[2]),
        pltpu.make_async_copy(rev, inputs.at[pl.ds(levels, top)], load_sem.at[3]),
    ]
    own_load.start()
    for load in in_loads:
        load.start()

    barrier = pltpu.get_barrier_semaphore()
    team = [(a, b) for a in range(n_dp) for b in range(GROUP) if (a, b) != (0, 0)]

    def team_member(a, b):
        return lax.rem(dp + a, n_dp), lax.rem(r + b, GROUP)

    for a, b in team:
        to_dp, to_r = team_member(a, b)
        pl.semaphore_signal(barrier, inc=1, device_id=(to_dp, q * GROUP + to_r), device_id_type=MESH)
    for k in range(1, groups):
        to_q = lax.rem(q + k, groups)
        pl.semaphore_signal(barrier, inc=1, device_id=(dp, to_q * GROUP + r), device_id_type=MESH)
    pl.semaphore_wait(barrier, len(team) + groups - 1)

    def part(ref, c):
        return ref.at[:, pl.ds(pl.multiple_of(c * rows, rows), rows), :]

    def hop(kind, c):
        if kind == 0:
            src, slot, to = part(cot, c), 4 * half, partner
        elif kind == 1:
            src, slot, to = part(cot, c), 1 + 2 * core, sibling
        elif kind == 2:
            src, slot, to = part(dy.at[4 - 4 * half], c), 4 * half, me + 4 - 8 * half
        else:
            src, slot, to = part(dy.at[4 - 4 * core], c), 3 - 2 * core, sibling
        return pltpu.make_async_remote_copy(
            src_ref=src,
            dst_ref=part(dy.at[slot], c),
            send_sem=send_sem.at[kind, c],
            recv_sem=recv_sem.at[kind, c],
            device_id=(dp, to),
            device_id_type=MESH,
        )

    @pl.loop(0, chunks)
    def _(c):
        hop(0, c).start()
        hop(1, c).start()

    @pl.when(jnp.logical_not(z_recvs))
    def _():
        dy[4 * half] = jnp.zeros(dy.shape[1:], dy.dtype)

    @pl.when(jnp.logical_and(jnp.logical_not(z_recvs), outer))
    def _():
        dy[1 + 2 * core] = jnp.zeros(dy.shape[1:], dy.dtype)

    per = 4 + 2 * top
    for b in range(2):
        f00, f01 = filt[b, 0, 0:1, :], filt[b, 0, 1:2, :]
        f10, f11 = filt[b, 1, 0:1, :], filt[b, 1, 1:2, :]
        last, w = mix[b, levels : levels + 1, :], mix[b, top : top + 1, :]
        values = [f01, f00, f01 * last + f11 * w, f00 * last + f10 * w]
        for level in range(top):
            w = mix[b, level : level + 1, :]
            values += [f11 * w, f10 * w]
        for k, value in enumerate(values):
            coef[b * per + k : b * per + k + 1, :] = value
    sums[...] = jnp.zeros(sums.shape, F32)

    n_sums = 2 + 4 * top

    def strip(row, lane):
        rows_at = pl.ds(pl.multiple_of(row, STRIP), STRIP)
        lanes_at = pl.ds(pl.multiple_of(lane, LANES), LANES)
        final = [None] * units
        for b in range(2):

            def place(m):
                return m % units if b == 0 else units - 1 - m % units

            def dy_at(m):
                block = 2 + m // units if b == 0 else 2 - m // units
                return dy[block, place(m), rows_at, lanes_at].astype(F32)

            def input_at(level, m):
                slot = 0 if level == 0 else (level if b == 0 else level + top)
                return inputs[slot, place(m), rows_at, lanes_at].astype(F32)

            def factor_at(k):
                return coef[b * per + k : b * per + k + 1, lanes_at]

            def add(k, value):
                sums[b * n_sums + k, :, lanes_at] += value

            shift = 2**top
            y = [dy_at(m) for m in range(units + 2 * shift - 1)]
            s_y = t_y = None
            for m in range(units):
                p = input_at(top, m)
                s, t = y[m + shift] * p, y[m] * p
                s_y = s if s_y is None else s_y + s
                t_y = t if t_y is None else t_y + t
            add(0, s_y)
            add(1, t_y)
            here, there = factor_at(2), factor_at(3)
            g = [here * y[m] + there * y[m + shift] for m in range(units + shift - 1)]
            for level in reversed(range(top)):
                shift = 2**level
                y = [dy_at(m) for m in range(units + 2 * shift - 1)]
                acc = None
                for m in range(units):
                    p = input_at(level, m)
                    terms = [g[m + shift] * p, y[m + shift] * p, g[m] * p, y[m] * p]
                    acc = terms if acc is None else [u + v for u, v in zip(acc, terms)]
                for k in range(4):
                    add(2 + 4 * level + k, acc[k])
                f01, f00 = factor_at(0), factor_at(1)
                w1, w0 = factor_at(4 + 2 * level), factor_at(5 + 2 * level)
                g = [
                    f01 * g[m] + w1 * y[m] + (f00 * g[m + shift] + w0 * y[m + shift])
                    for m in range(units + shift - 1)
                ]
            for m in range(units):
                final[place(m)] = g[m] if b == 0 else final[place(m)] + g[m]
        for j in range(units):
            result[j, rows_at, lanes_at] = final[j].astype(result.dtype)

    def store(c):
        return pltpu.make_async_copy(part(result, c), part(out, c), store_sem.at[c])

    own_load.wait()
    for load in in_loads:
        load.wait()

    lane_blocks = width // LANES
    pieces = (rows // STRIP) * lane_blocks

    @pl.loop(0, chunks + 2)
    def _(step):
        @pl.when(step < chunks)
        def _():
            hop(0, step).wait_recv()

            @pl.when(z_sends)
            def _():
                hop(2, step).start()

            @pl.when(outer)
            def _():
                hop(3, step).start()

        @pl.when(jnp.logical_and(step >= 1, step < chunks + 1))
        def _():
            c = step - 1

            @pl.when(z_recvs)
            def _():
                hop(2, c).wait_recv()

                @pl.when(jnp.logical_not(outer))
                def _():
                    hop(3, c).start()

        @pl.when(step >= 2)
        def _():
            c = step - 2
            hop(1, c).wait_recv()

            @pl.when(jnp.logical_or(jnp.logical_not(outer), z_recvs))
            def _():
                hop(3, c).wait_recv()

            @pl.loop(0, pieces)
            def _(piece):
                strip(c * rows + lax.div(piece, lane_blocks) * STRIP, lax.rem(piece, lane_blocks) * LANES)

            store(c).start()

    slot_a = dp * GROUP + r
    n_filt = 8
    for b in range(2):
        f00, f01 = filt[b, 0, 0:1, :], filt[b, 0, 1:2, :]
        f10, f11 = filt[b, 1, 0:1, :], filt[b, 1, 1:2, :]

        def total(k):
            return jnp.sum(sums[b * n_sums + k], axis=0, keepdims=True)

        def put(k, value):
            buf_a[slot_a, k : k + 1, :] = value

        s_y, t_y = total(0), total(1)
        last, w = mix[b, levels : levels + 1, :], mix[b, top : top + 1, :]
        terms = [last * s_y, last * t_y, w * s_y, w * t_y]
        base = n_filt + b * (levels + 1)
        put(base + levels, f00 * s_y + f01 * t_y)
        put(base + top, f10 * s_y + f11 * t_y)
        for level in reversed(range(top)):
            s_a, s_y, t_a, t_y = [total(2 + 4 * level + k) for k in range(4)]
            w = mix[b, level : level + 1, :]
            terms = [u + v for u, v in zip(terms, [s_a, t_a, w * s_y, w * t_y])]
            put(base + level, f10 * s_y + f11 * t_y)
        for k in range(4):
            put(4 * b + k, terms[k])

    def team_copy(a, b):
        to_dp, to_r = team_member(a, b)
        slot = dp * GROUP + r
        return pltpu.make_async_remote_copy(
            src_ref=buf_a.at[slot],
            dst_ref=buf_a.at[slot],
            send_sem=send_a.at[a * GROUP + b],
            recv_sem=recv_a.at[a * GROUP + b],
            device_id=(to_dp, q * GROUP + to_r),
            device_id_type=MESH,
        )

    def group_copy(k):
        to_q = lax.rem(q + k, groups)
        return pltpu.make_async_remote_copy(
            src_ref=buf_b.at[q],
            dst_ref=buf_b.at[q],
            send_sem=send_b.at[k],
            recv_sem=recv_b.at[k],
            device_id=(dp, to_q * GROUP + r),
            device_id_type=MESH,
        )

    for a, b in team:
        team_copy(a, b).start()
    for a, b in team:
        team_copy(a, b).wait_recv()
    value = buf_a[0]
    for k in range(1, n_dp * GROUP):
        value = value + buf_a[k]
    buf_b[q] = value
    for k in range(1, groups):
        group_copy(k).start()
    for k in range(1, groups):
        group_copy(k).wait_recv()
    value = buf_b[0]
    for k in range(1, groups):
        value = value + buf_b[k]
    value = value * factor
    for b in range(2):
        for kind in range(2):
            at = 4 * b + 2 * kind
            out_filt[b, kind] = value[at : at + 2]
        base = n_filt + b * (levels + 1)
        out_mix[b] = value[base : base + levels + 1]

    for a, b in team:
        team_copy(a, b).wait_send()
    for k in range(1, groups):
        group_copy(k).wait_send()

    @pl.loop(0, chunks)
    def _(c):
        hop(0, c).wait_send()
        hop(1, c).wait_send()
        store(c).wait()

        @pl.when(z_sends)
        def _():
            hop(2, c).wait_send()

        @pl.when(jnp.logical_or(outer, z_recvs))
        def _():
            hop(3, c).wait_send()


def body(level_input, saved_forward, saved_reverse, filters, mixing, cotangent):
    n_dp, n_ctx = lax.axis_size("dp"), lax.axis_size("ctx")
    levels = saved_forward.shape[0] + 1
    seqs, span, width = level_input.shape
    units = span // BASE
    assert seqs == 1 and span % BASE == 0 and n_ctx % GROUP == 0
    assert 2**levels <= 2 * units and width % LANES == 0
    rows = STRIP
    chunks = BASE // rows
    top = levels - 1
    groups = n_ctx // GROUP
    factor = 1.0 / math.sqrt(seqs * n_dp * span * n_ctx)
    terms = 8 + 2 * (levels + 1)
    block = (units, BASE, width)
    dma = pltpu.SemaphoreType.DMA
    anywhere = pl.BlockSpec(memory_space=pl.ANY)
    vmem = pl.BlockSpec(memory_space=pltpu.VMEM)
    grad_input, grad_filters, grad_mixing = pl.pallas_call(
        functools.partial(kernel, (n_dp, n_ctx, units, levels, rows, factor)),
        out_shape=(
            jax.ShapeDtypeStruct(block, jnp.bfloat16),
            jax.ShapeDtypeStruct(filters.shape, F32),
            jax.ShapeDtypeStruct(mixing.shape, F32),
        ),
        in_specs=[anywhere] * 4 + [vmem] * 2,
        out_specs=(anywhere, vmem, vmem),
        scratch_shapes=[
            pltpu.VMEM((5,) + block, jnp.bfloat16),
            pltpu.VMEM((2 * levels - 1,) + block, jnp.bfloat16),
            pltpu.VMEM(block, jnp.bfloat16),
            pltpu.VMEM((2 * (2 + 4 * top), STRIP, width), F32),
            pltpu.VMEM((2 * (4 + 2 * top), width), F32),
            pltpu.VMEM((n_dp * GROUP, terms, width), F32),
            pltpu.VMEM((groups, terms, width), F32),
            dma((4,)),
            dma((chunks,)),
            dma((4, chunks)),
            dma((4, chunks)),
            dma((n_dp * GROUP,)),
            dma((n_dp * GROUP,)),
            dma((groups,)),
            dma((groups,)),
        ],
        compiler_params=pltpu.CompilerParams(
            collective_id=0, has_side_effects=True, vmem_limit_bytes=32 * 1024 * 1024
        ),
        cost_estimate=pl.CostEstimate(
            flops=300 * span * width, bytes_accessed=9 * span * width * 2, transcendentals=0
        ),
    )(
        cotangent.reshape(block),
        level_input.reshape(block),
        saved_forward.reshape((top,) + block),
        saved_reverse.reshape((top,) + block),
        filters,
        mixing,
    )
    return (grad_input.reshape(level_input.shape), grad_filters, grad_mixing)


def solution(mesh):
    return jax.shard_map(
        body,
        mesh=mesh,
        in_specs=(
            P("dp", "ctx", None),
            P(None, "dp", "ctx", None),
            P(None, "dp", "ctx", None),
            P(),
            P(),
            P("dp", "ctx", None),
        ),
        out_specs=(P("dp", "ctx", None), P(), P()),
        check_vma=False,
    )
```

```python
import functools
import math

import jax
import jax.numpy as jnp
from jax import lax
from jax.experimental import pallas as pl
from jax.experimental.pallas import tpu as pltpu
from jax.sharding import PartitionSpec as P

BASE = 128
STRIP = 16
LANES = 128
GROUP = 4
MESH = pl.DeviceIdType.MESH
F32 = jnp.float32


def kernel(
    dims,
    cot,
    first,
    fwd,
    rev,
    filt_in,
    mix_in,
    out,
    out_filt,
    out_mix,
    dy,
    inputs,
    filt,
    mix,
    result,
    sums,
    coef,
    buf_a,
    buf_b,
    load_sem,
    store_sem,
    send_sem,
    recv_sem,
    send_a,
    recv_a,
    send_b,
    recv_b,
):
    n_dp, n_ctx, units, levels, rows, factor = dims
    chunks = BASE // rows
    groups = n_ctx // GROUP
    width = dy.shape[-1]
    top = levels - 1

    dp = lax.axis_index("dp")
    me = lax.axis_index("ctx")
    q = lax.div(me, GROUP)
    r = lax.rem(me, GROUP)
    half = lax.div(r, 2)
    core = lax.rem(r, 2)
    outer = half == core
    sibling = me + 1 - 2 * core
    partner = me + 2 - 4 * half
    has_next = q < groups - 1
    has_prev = q > 0
    lower = half == 0
    z_sends = jnp.logical_or(jnp.logical_and(lower, has_next), jnp.logical_and(half == 1, has_prev))
    z_recvs = jnp.logical_or(jnp.logical_and(lower, has_prev), jnp.logical_and(half == 1, has_next))

    own_load = pltpu.make_async_copy(cot, dy.at[2], load_sem.at[0])
    in_loads = [
        pltpu.make_async_copy(first, inputs.at[0], load_sem.at[1]),
        pltpu.make_async_copy(fwd, inputs.at[pl.ds(1, top)], load_sem.at[2]),
        pltpu.make_async_copy(rev, inputs.at[pl.ds(levels, top)], load_sem.at[3]),
    ]
    small_loads = [
        pltpu.make_async_copy(filt_in, filt, load_sem.at[4]),
        pltpu.make_async_copy(mix_in, mix, load_sem.at[5]),
    ]
    for load in small_loads + [own_load] + in_loads:
        load.start()

    barrier = pltpu.get_barrier_semaphore()
    team = [(a, b) for a in range(n_dp) for b in range(GROUP) if (a, b) != (0, 0)]

    def team_member(a, b):
        return lax.rem(dp + a, n_dp), lax.rem(r + b, GROUP)

    for a, b in team:
        to_dp, to_r = team_member(a, b)
        pl.semaphore_signal(barrier, inc=1, device_id=(to_dp, q * GROUP + to_r), device_id_type=MESH)
    for k in range(1, groups):
        to_q = lax.rem(q + k, groups)
        pl.semaphore_signal(barrier, inc=1, device_id=(dp, to_q * GROUP + r), device_id_type=MESH)
    pl.semaphore_wait(barrier, len(team) + groups - 1)

    def part(ref, c):
        return ref.at[:, pl.ds(pl.multiple_of(c * rows, rows), rows), :]

    def hop(kind, c):
        if kind == 0:
            src, slot, to = part(cot, c), 4 * half, partner
        elif kind == 1:
            src, slot, to = part(cot, c), 1 + 2 * core, sibling
        elif kind == 2:
            src, slot, to = part(dy.at[4 - 4 * half], c), 4 * half, me + 4 - 8 * half
        else:
            src, slot, to = part(dy.at[4 - 4 * core], c), 3 - 2 * core, sibling
        return pltpu.make_async_remote_copy(
            src_ref=src,
            dst_ref=part(dy.at[slot], c),
            send_sem=send_sem.at[kind, c],
            recv_sem=recv_sem.at[kind, c],
            device_id=(dp, to),
            device_id_type=MESH,
        )

    @pl.loop(0, chunks)
    def _(c):
        hop(0, c).start()
        hop(1, c).start()

    @pl.when(jnp.logical_not(z_recvs))
    def _():
        dy[4 * half] = jnp.zeros(dy.shape[1:], dy.dtype)

    @pl.when(jnp.logical_and(jnp.logical_not(z_recvs), outer))
    def _():
        dy[1 + 2 * core] = jnp.zeros(dy.shape[1:], dy.dtype)

    for load in small_loads:
        load.wait()

    def weight(b, level):
        return mix[level, b : b + 1, :]

    per = 4 + 2 * top
    for b in range(2):
        f00, f01 = filt[b, 0, 0:1, :], filt[b, 0, 1:2, :]
        f10, f11 = filt[b, 1, 0:1, :], filt[b, 1, 1:2, :]
        last, w = weight(b, levels), weight(b, top)
        values = [f01, f00, f01 * last + f11 * w, f00 * last + f10 * w]
        for level in range(top):
            w = weight(b, level)
            values += [f11 * w, f10 * w]
        for k, value in enumerate(values):
            coef[b * per + k : b * per + k + 1, :] = value
    sums[...] = jnp.zeros(sums.shape, F32)

    n_sums = 2 + 4 * top

    def strip(row, lane):
        rows_at = pl.ds(pl.multiple_of(row, STRIP), STRIP)
        lanes_at = pl.ds(pl.multiple_of(lane, LANES), LANES)
        final = [None] * units
        for b in range(2):

            def place(m):
                return m % units if b == 0 else units - 1 - m % units

            def dy_at(m):
                block = 2 + m // units if b == 0 else 2 - m // units
                return dy[block, place(m), rows_at, lanes_at].astype(F32)

            def input_at(level, m):
                slot = 0 if level == 0 else (level if b == 0 else level + top)
                return inputs[slot, place(m), rows_at, lanes_at].astype(F32)

            def factor_at(k):
                return coef[b * per + k : b * per + k + 1, lanes_at]

            def add(k, value):
                sums[b * n_sums + k, :, lanes_at] += value

            shift = 2**top
            y = [dy_at(m) for m in range(units + 2 * shift - 1)]
            s_y = t_y = None
            for m in range(units):
                p = input_at(top, m)
                s, t = y[m + shift] * p, y[m] * p
                s_y = s if s_y is None else s_y + s
                t_y = t if t_y is None else t_y + t
            add(0, s_y)
            add(1, t_y)
            here, there = factor_at(2), factor_at(3)
            g = [here * y[m] + there * y[m + shift] for m in range(units + shift - 1)]
            for level in reversed(range(top)):
                shift = 2**level
                y = [dy_at(m) for m in range(units + 2 * shift - 1)]
                acc = None
                for m in range(units):
                    p = input_at(level, m)
                    terms = [g[m + shift] * p, y[m + shift] * p, g[m] * p, y[m] * p]
                    acc = terms if acc is None else [u + v for u, v in zip(acc, terms)]
                for k in range(4):
                    add(2 + 4 * level + k, acc[k])
                f01, f00 = factor_at(0), factor_at(1)
                w1, w0 = factor_at(4 + 2 * level), factor_at(5 + 2 * level)
                g = [
                    f01 * g[m] + w1 * y[m] + (f00 * g[m + shift] + w0 * y[m + shift])
                    for m in range(units + shift - 1)
                ]
            for m in range(units):
                final[place(m)] = g[m] if b == 0 else final[place(m)] + g[m]
        for j in range(units):
            result[j, rows_at, lanes_at] = final[j].astype(result.dtype)

    def store(c):
        return pltpu.make_async_copy(part(result, c), part(out, c), store_sem.at[c])

    own_load.wait()
    for load in in_loads:
        load.wait()

    lane_blocks = width // LANES
    mid, late = 2, 3
    pieces = (rows // STRIP) * lane_blocks

    @pl.loop(0, chunks + late)
    def _(step):
        @pl.when(step < chunks)
        def _():
            hop(0, step).wait_recv()

            @pl.when(z_sends)
            def _():
                hop(2, step).start()

            @pl.when(outer)
            def _():
                hop(3, step).start()

        @pl.when(jnp.logical_and(step >= mid, step < chunks + mid))
        def _():
            c = step - mid

            @pl.when(z_recvs)
            def _():
                hop(2, c).wait_recv()

                @pl.when(jnp.logical_not(outer))
                def _():
                    hop(3, c).start()

        @pl.when(step >= late)
        def _():
            c = step - late
            hop(1, c).wait_recv()

            @pl.when(jnp.logical_or(jnp.logical_not(outer), z_recvs))
            def _():
                hop(3, c).wait_recv()

            @pl.loop(0, pieces)
            def _(piece):
                strip(c * rows + lax.div(piece, lane_blocks) * STRIP, lax.rem(piece, lane_blocks) * LANES)

            store(c).start()

    slot_a = dp * GROUP + r
    n_filt = 8
    for b in range(2):
        f00, f01 = filt[b, 0, 0:1, :], filt[b, 0, 1:2, :]
        f10, f11 = filt[b, 1, 0:1, :], filt[b, 1, 1:2, :]

        def total(k):
            return jnp.sum(sums[b * n_sums + k], axis=0, keepdims=True)

        def put(k, value):
            buf_a[slot_a, k : k + 1, :] = value

        s_y, t_y = total(0), total(1)
        last, w = weight(b, levels), weight(b, top)
        terms = [last * s_y, last * t_y, w * s_y, w * t_y]
        base = n_filt + b * (levels + 1)
        put(base + levels, f00 * s_y + f01 * t_y)
        put(base + top, f10 * s_y + f11 * t_y)
        for level in reversed(range(top)):
            s_a, s_y, t_a, t_y = [total(2 + 4 * level + k) for k in range(4)]
            w = weight(b, level)
            terms = [u + v for u, v in zip(terms, [s_a, t_a, w * s_y, w * t_y])]
            put(base + level, f10 * s_y + f11 * t_y)
        for k in range(4):
            put(4 * b + k, terms[k])

    def team_copy(a, b):
        to_dp, to_r = team_member(a, b)
        slot = dp * GROUP + r
        return pltpu.make_async_remote_copy(
            src_ref=buf_a.at[slot],
            dst_ref=buf_a.at[slot],
            send_sem=send_a.at[a * GROUP + b],
            recv_sem=recv_a.at[a * GROUP + b],
            device_id=(to_dp, q * GROUP + to_r),
            device_id_type=MESH,
        )

    def group_copy(k):
        to_q = lax.rem(q + k, groups)
        return pltpu.make_async_remote_copy(
            src_ref=buf_b.at[q],
            dst_ref=buf_b.at[q],
            send_sem=send_b.at[k],
            recv_sem=recv_b.at[k],
            device_id=(dp, to_q * GROUP + r),
            device_id_type=MESH,
        )

    for a, b in team:
        team_copy(a, b).start()
    for a, b in team:
        team_copy(a, b).wait_recv()
    value = buf_a[0]
    for k in range(1, n_dp * GROUP):
        value = value + buf_a[k]
    buf_b[q] = value
    for k in range(1, groups):
        group_copy(k).start()
    for k in range(1, groups):
        group_copy(k).wait_recv()
    value = buf_b[0]
    for k in range(1, groups):
        value = value + buf_b[k]
    value = value * factor
    for b in range(2):
        for kind in range(2):
            at = 4 * b + 2 * kind
            out_filt[b, kind] = value[at : at + 2]
        base = n_filt + b * (levels + 1)
        out_mix[:, b] = value[base : base + levels + 1]

    for a, b in team:
        team_copy(a, b).wait_send()
    for k in range(1, groups):
        group_copy(k).wait_send()

    @pl.loop(0, chunks)
    def _(c):
        hop(0, c).wait_send()
        hop(1, c).wait_send()
        store(c).wait()

        @pl.when(z_sends)
        def _():
            hop(2, c).wait_send()

        @pl.when(jnp.logical_or(outer, z_recvs))
        def _():
            hop(3, c).wait_send()


def body(level_input, saved_forward, saved_reverse, filters, mixing, cotangent):
    n_dp, n_ctx = lax.axis_size("dp"), lax.axis_size("ctx")
    levels = saved_forward.shape[0] + 1
    seqs, span, width = level_input.shape
    units = span // BASE
    assert seqs == 1 and span % BASE == 0 and n_ctx % GROUP == 0
    assert 2**levels <= 2 * units and width % LANES == 0
    rows = STRIP
    chunks = BASE // rows
    top = levels - 1
    groups = n_ctx // GROUP
    factor = 1.0 / math.sqrt(seqs * n_dp * span * n_ctx)
    terms = 8 + 2 * (levels + 1)
    block = (units, BASE, width)
    by_level = mixing.transpose(1, 0, 2)
    dma = pltpu.SemaphoreType.DMA
    hbm = pl.BlockSpec(memory_space=pltpu.HBM)
    vmem = pl.BlockSpec(memory_space=pltpu.VMEM)
    grad_input, grad_filters, grad_mixing = pl.pallas_call(
        functools.partial(kernel, (n_dp, n_ctx, units, levels, rows, factor)),
        out_shape=(
            jax.ShapeDtypeStruct(block, jnp.bfloat16),
            jax.ShapeDtypeStruct(filters.shape, F32),
            jax.ShapeDtypeStruct(by_level.shape, F32),
        ),
        in_specs=[hbm] * 6,
        out_specs=(hbm, vmem, vmem),
        scratch_shapes=[
            pltpu.VMEM((5,) + block, jnp.bfloat16),
            pltpu.VMEM((2 * levels - 1,) + block, jnp.bfloat16),
            pltpu.VMEM(filters.shape, F32),
            pltpu.VMEM(by_level.shape, F32),
            pltpu.VMEM(block, jnp.bfloat16),
            pltpu.VMEM((2 * (2 + 4 * top), STRIP, width), F32),
            pltpu.VMEM((2 * (4 + 2 * top), width), F32),
            pltpu.VMEM((n_dp * GROUP, terms, width), F32),
            pltpu.VMEM((groups, terms, width), F32),
            dma((6,)),
            dma((chunks,)),
            dma((4, chunks)),
            dma((4, chunks)),
            dma((n_dp * GROUP,)),
            dma((n_dp * GROUP,)),
            dma((groups,)),
            dma((groups,)),
        ],
        compiler_params=pltpu.CompilerParams(
            collective_id=0, has_side_effects=True, vmem_limit_bytes=63 * 1024 * 1024
        ),
        cost_estimate=pl.CostEstimate(
            flops=300 * span * width, bytes_accessed=9 * span * width * 2, transcendentals=0
        ),
    )(
        cotangent.reshape(block),
        level_input.reshape(block),
        saved_forward.reshape((top,) + block),
        saved_reverse.reshape((top,) + block),
        filters,
        by_level,
    )
    return (grad_input.reshape(level_input.shape), grad_filters, grad_mixing.transpose(1, 0, 2))


def solution(mesh):
    return jax.shard_map(
        body,
        mesh=mesh,
        in_specs=(
            P("dp", "ctx", None),
            P(None, "dp", "ctx", None),
            P(None, "dp", "ctx", None),
            P(),
            P(),
            P("dp", "ctx", None),
        ),
        out_specs=(P("dp", "ctx", None), P(), P()),
        check_vma=False,
    )
```

```python
import functools
import math

import jax
import jax.numpy as jnp
from jax import lax
from jax.experimental import pallas as pl
from jax.experimental.pallas import tpu as pltpu
from jax.sharding import PartitionSpec as P

BASE = 128
STRIP = 16
LANES = 128
GROUP = 4
MESH = pl.DeviceIdType.MESH
F32 = jnp.float32


def kernel(
    dims,
    cot,
    first,
    fwd,
    rev,
    filt_in,
    mix_in,
    out,
    out_filt,
    out_mix,
    dy,
    inputs,
    filt,
    mix,
    sums,
    coef,
    buf_a,
    buf_b,
    load_sem,
    send_sem,
    recv_sem,
    send_a,
    recv_a,
    send_b,
    recv_b,
):
    n_dp, n_ctx, units, levels, rows, factor = dims
    chunks = BASE // rows
    groups = n_ctx // GROUP
    width = dy.shape[-1]
    top = levels - 1

    dp = lax.axis_index("dp")
    me = lax.axis_index("ctx")
    q = lax.div(me, GROUP)
    r = lax.rem(me, GROUP)
    half = lax.div(r, 2)
    core = lax.rem(r, 2)
    outer = half == core
    sibling = me + 1 - 2 * core
    partner = me + 2 - 4 * half
    has_next = q < groups - 1
    has_prev = q > 0
    lower = half == 0
    z_sends = jnp.logical_or(jnp.logical_and(lower, has_next), jnp.logical_and(half == 1, has_prev))
    z_recvs = jnp.logical_or(jnp.logical_and(lower, has_prev), jnp.logical_and(half == 1, has_next))

    own_load = pltpu.make_async_copy(cot, dy.at[2], load_sem.at[0])
    in_loads = [
        pltpu.make_async_copy(first, inputs.at[0], load_sem.at[1]),
        pltpu.make_async_copy(fwd, inputs.at[pl.ds(1, top)], load_sem.at[2]),
        pltpu.make_async_copy(rev, inputs.at[pl.ds(levels, top)], load_sem.at[3]),
    ]
    small_loads = [
        pltpu.make_async_copy(filt_in, filt, load_sem.at[4]),
        pltpu.make_async_copy(mix_in, mix, load_sem.at[5]),
    ]
    for load in small_loads + [own_load] + in_loads:
        load.start()

    barrier = pltpu.get_barrier_semaphore()
    team = [(a, b) for a in range(n_dp) for b in range(GROUP) if (a, b) != (0, 0)]

    def team_member(a, b):
        return lax.rem(dp + a, n_dp), lax.rem(r + b, GROUP)

    for a, b in team:
        to_dp, to_r = team_member(a, b)
        pl.semaphore_signal(barrier, inc=1, device_id=(to_dp, q * GROUP + to_r), device_id_type=MESH)
    for k in range(1, groups):
        to_q = lax.rem(q + k, groups)
        pl.semaphore_signal(barrier, inc=1, device_id=(dp, to_q * GROUP + r), device_id_type=MESH)
    pl.semaphore_wait(barrier, len(team) + groups - 1)

    def part(ref, c):
        return ref.at[:, pl.ds(pl.multiple_of(c * rows, rows), rows), :]

    def hop(kind, c):
        if kind == 0:
            src, slot, to = part(cot, c), 4 * half, partner
        elif kind == 1:
            src, slot, to = part(cot, c), 1 + 2 * core, sibling
        elif kind == 2:
            src, slot, to = part(dy.at[4 - 4 * half], c), 4 * half, me + 4 - 8 * half
        else:
            src, slot, to = part(dy.at[4 - 4 * core], c), 3 - 2 * core, sibling
        return pltpu.make_async_remote_copy(
            src_ref=src,
            dst_ref=part(dy.at[slot], c),
            send_sem=send_sem.at[kind, c],
            recv_sem=recv_sem.at[kind, c],
            device_id=(dp, to),
            device_id_type=MESH,
        )

    @pl.loop(0, chunks)
    def _(c):
        hop(0, c).start()
        hop(1, c).start()

    @pl.when(jnp.logical_not(z_recvs))
    def _():
        dy[4 * half] = jnp.zeros(dy.shape[1:], dy.dtype)

    @pl.when(jnp.logical_and(jnp.logical_not(z_recvs), outer))
    def _():
        dy[1 + 2 * core] = jnp.zeros(dy.shape[1:], dy.dtype)

    for load in small_loads:
        load.wait()

    def weight(b, level):
        return mix[level, b : b + 1, :]

    per = 4 + 2 * top
    for b in range(2):
        f00, f01 = filt[b, 0, 0:1, :], filt[b, 0, 1:2, :]
        f10, f11 = filt[b, 1, 0:1, :], filt[b, 1, 1:2, :]
        last, w = weight(b, levels), weight(b, top)
        values = [f01, f00, f01 * last + f11 * w, f00 * last + f10 * w]
        for level in range(top):
            w = weight(b, level)
            values += [f11 * w, f10 * w]
        for k, value in enumerate(values):
            coef[b * per + k : b * per + k + 1, :] = value
    sums[...] = jnp.zeros(sums.shape, F32)

    n_sums = 2 + 4 * top

    def strip(row, lane):
        rows_at = pl.ds(pl.multiple_of(row, STRIP), STRIP)
        lanes_at = pl.ds(pl.multiple_of(lane, LANES), LANES)
        final = [None] * units
        for b in range(2):

            def place(m):
                return m % units if b == 0 else units - 1 - m % units

            def dy_at(m):
                block = 2 + m // units if b == 0 else 2 - m // units
                return dy[block, place(m), rows_at, lanes_at].astype(F32)

            def input_at(level, m):
                slot = 0 if level == 0 else (level if b == 0 else level + top)
                return inputs[slot, place(m), rows_at, lanes_at].astype(F32)

            def factor_at(k):
                return coef[b * per + k : b * per + k + 1, lanes_at]

            def add(k, value):
                sums[b * n_sums + k, :, lanes_at] += value

            shift = 2**top
            y = [dy_at(m) for m in range(units + 2 * shift - 1)]
            s_y = t_y = None
            for m in range(units):
                p = input_at(top, m)
                s, t = y[m + shift] * p, y[m] * p
                s_y = s if s_y is None else s_y + s
                t_y = t if t_y is None else t_y + t
            add(0, s_y)
            add(1, t_y)
            here, there = factor_at(2), factor_at(3)
            g = [here * y[m] + there * y[m + shift] for m in range(units + shift - 1)]
            for level in reversed(range(top)):
                shift = 2**level
                y = [dy_at(m) for m in range(units + 2 * shift - 1)]
                acc = None
                for m in range(units):
                    p = input_at(level, m)
                    terms = [g[m + shift] * p, y[m + shift] * p, g[m] * p, y[m] * p]
                    acc = terms if acc is None else [u + v for u, v in zip(acc, terms)]
                for k in range(4):
                    add(2 + 4 * level + k, acc[k])
                f01, f00 = factor_at(0), factor_at(1)
                w1, w0 = factor_at(4 + 2 * level), factor_at(5 + 2 * level)
                g = [
                    f01 * g[m] + w1 * y[m] + (f00 * g[m + shift] + w0 * y[m + shift])
                    for m in range(units + shift - 1)
                ]
            for m in range(units):
                final[place(m)] = g[m] if b == 0 else final[place(m)] + g[m]
        for j in range(units):
            out[j, rows_at, lanes_at] = final[j].astype(out.dtype)

    own_load.wait()
    for load in in_loads:
        load.wait()

    lane_blocks = width // LANES
    mid, late = 2, 3
    pieces = (rows // STRIP) * lane_blocks

    @pl.loop(0, chunks + late)
    def _(step):
        @pl.when(step < chunks)
        def _():
            hop(0, step).wait_recv()

            @pl.when(z_sends)
            def _():
                hop(2, step).start()

            @pl.when(outer)
            def _():
                hop(3, step).start()

        @pl.when(jnp.logical_and(step >= mid, step < chunks + mid))
        def _():
            c = step - mid

            @pl.when(z_recvs)
            def _():
                hop(2, c).wait_recv()

                @pl.when(jnp.logical_not(outer))
                def _():
                    hop(3, c).start()

        @pl.when(step >= late)
        def _():
            c = step - late
            hop(1, c).wait_recv()

            @pl.when(jnp.logical_or(jnp.logical_not(outer), z_recvs))
            def _():
                hop(3, c).wait_recv()

            @pl.loop(0, pieces)
            def _(piece):
                strip(c * rows + lax.div(piece, lane_blocks) * STRIP, lax.rem(piece, lane_blocks) * LANES)

    slot_a = dp * GROUP + r
    n_filt = 8
    for b in range(2):
        f00, f01 = filt[b, 0, 0:1, :], filt[b, 0, 1:2, :]
        f10, f11 = filt[b, 1, 0:1, :], filt[b, 1, 1:2, :]

        def total(k):
            return jnp.sum(sums[b * n_sums + k], axis=0, keepdims=True)

        def put(k, value):
            buf_a[slot_a, k : k + 1, :] = value

        s_y, t_y = total(0), total(1)
        last, w = weight(b, levels), weight(b, top)
        terms = [last * s_y, last * t_y, w * s_y, w * t_y]
        base = n_filt + b * (levels + 1)
        put(base + levels, f00 * s_y + f01 * t_y)
        put(base + top, f10 * s_y + f11 * t_y)
        for level in reversed(range(top)):
            s_a, s_y, t_a, t_y = [total(2 + 4 * level + k) for k in range(4)]
            w = weight(b, level)
            terms = [u + v for u, v in zip(terms, [s_a, t_a, w * s_y, w * t_y])]
            put(base + level, f10 * s_y + f11 * t_y)
        for k in range(4):
            put(4 * b + k, terms[k])

    def team_copy(a, b):
        to_dp, to_r = team_member(a, b)
        slot = dp * GROUP + r
        return pltpu.make_async_remote_copy(
            src_ref=buf_a.at[slot],
            dst_ref=buf_a.at[slot],
            send_sem=send_a.at[a * GROUP + b],
            recv_sem=recv_a.at[a * GROUP + b],
            device_id=(to_dp, q * GROUP + to_r),
            device_id_type=MESH,
        )

    def group_copy(k):
        to_q = lax.rem(q + k, groups)
        return pltpu.make_async_remote_copy(
            src_ref=buf_b.at[q],
            dst_ref=buf_b.at[q],
            send_sem=send_b.at[k],
            recv_sem=recv_b.at[k],
            device_id=(dp, to_q * GROUP + r),
            device_id_type=MESH,
        )

    for a, b in team:
        team_copy(a, b).start()
    for a, b in team:
        team_copy(a, b).wait_recv()
    value = buf_a[0]
    for k in range(1, n_dp * GROUP):
        value = value + buf_a[k]
    buf_b[q] = value
    for k in range(1, groups):
        group_copy(k).start()
    for k in range(1, groups):
        group_copy(k).wait_recv()
    value = buf_b[0]
    for k in range(1, groups):
        value = value + buf_b[k]
    value = value * factor
    for b in range(2):
        for kind in range(2):
            at = 4 * b + 2 * kind
            out_filt[b, kind] = value[at : at + 2]
        base = n_filt + b * (levels + 1)
        out_mix[:, b] = value[base : base + levels + 1]

    for a, b in team:
        team_copy(a, b).wait_send()
    for k in range(1, groups):
        group_copy(k).wait_send()

    @pl.loop(0, chunks)
    def _(c):
        hop(0, c).wait_send()
        hop(1, c).wait_send()

        @pl.when(z_sends)
        def _():
            hop(2, c).wait_send()

        @pl.when(jnp.logical_or(outer, z_recvs))
        def _():
            hop(3, c).wait_send()


def body(level_input, saved_forward, saved_reverse, filters, mixing, cotangent):
    n_dp, n_ctx = lax.axis_size("dp"), lax.axis_size("ctx")
    levels = saved_forward.shape[0] + 1
    seqs, span, width = level_input.shape
    units = span // BASE
    assert seqs == 1 and span % BASE == 0 and n_ctx % GROUP == 0
    assert 2**levels <= 2 * units and width % LANES == 0
    rows = STRIP
    chunks = BASE // rows
    top = levels - 1
    groups = n_ctx // GROUP
    factor = 1.0 / math.sqrt(seqs * n_dp * span * n_ctx)
    terms = 8 + 2 * (levels + 1)
    block = (units, BASE, width)
    by_level = mixing.transpose(1, 0, 2)
    dma = pltpu.SemaphoreType.DMA
    hbm = pl.BlockSpec(memory_space=pltpu.HBM)
    vmem = pl.BlockSpec(memory_space=pltpu.VMEM)
    grad_input, grad_filters, grad_mixing = pl.pallas_call(
        functools.partial(kernel, (n_dp, n_ctx, units, levels, rows, factor)),
        out_shape=(
            pltpu.VMEM(block, jnp.bfloat16),
            pltpu.VMEM(filters.shape, F32),
            pltpu.VMEM(by_level.shape, F32),
        ),
        in_specs=[hbm] * 6,
        out_specs=(vmem, vmem, vmem),
        scratch_shapes=[
            pltpu.VMEM((5,) + block, jnp.bfloat16),
            pltpu.VMEM((2 * levels - 1,) + block, jnp.bfloat16),
            pltpu.VMEM(filters.shape, F32),
            pltpu.VMEM(by_level.shape, F32),
            pltpu.VMEM((2 * (2 + 4 * top), STRIP, width), F32),
            pltpu.VMEM((2 * (4 + 2 * top), width), F32),
            pltpu.VMEM((n_dp * GROUP, terms, width), F32),
            pltpu.VMEM((groups, terms, width), F32),
            dma((6,)),
            dma((4, chunks)),
            dma((4, chunks)),
            dma((n_dp * GROUP,)),
            dma((n_dp * GROUP,)),
            dma((groups,)),
            dma((groups,)),
        ],
        compiler_params=pltpu.CompilerParams(
            collective_id=0, has_side_effects=True, vmem_limit_bytes=32 * 1024 * 1024
        ),
        cost_estimate=pl.CostEstimate(
            flops=300 * span * width, bytes_accessed=9 * span * width * 2, transcendentals=0
        ),
    )(
        *[
            pltpu.with_memory_space_constraint(operand, pltpu.HBM)
            for operand in (
                cotangent.reshape(block),
                level_input.reshape(block),
                saved_forward.reshape((top,) + block),
                saved_reverse.reshape((top,) + block),
                filters,
                by_level,
            )
        ]
    )
    return (grad_input.reshape(level_input.shape), grad_filters, grad_mixing.transpose(1, 0, 2))


def solution(mesh):
    return jax.shard_map(
        body,
        mesh=mesh,
        in_specs=(
            P("dp", "ctx", None),
            P(None, "dp", "ctx", None),
            P(None, "dp", "ctx", None),
            P(),
            P(),
            P("dp", "ctx", None),
        ),
        out_specs=(P("dp", "ctx", None), P(), P()),
        check_vma=False,
    )
```

```python
import functools
import math

import jax
import jax.numpy as jnp
from jax import lax
from jax.experimental import pallas as pl
from jax.experimental.pallas import tpu as pltpu
from jax.sharding import PartitionSpec as P

BASE = 128
STRIP = 16
LANES = 128
GROUP = 4
MESH = pl.DeviceIdType.MESH
F32 = jnp.float32


def kernel(
    dims,
    cot,
    first,
    fwd,
    rev,
    filt_in,
    mix_in,
    out,
    out_filt,
    out_mix,
    dy,
    inputs,
    filt,
    mix,
    dy_wide,
    inputs_wide,
    halo,
    partial,
    plain_sums,
    sums,
    coef,
    buf_a,
    buf_b,
    load_sem,
    send_sem,
    recv_sem,
    send_a,
    recv_a,
    send_b,
    recv_b,
):
    n_dp, n_ctx, units, levels, rows, factor = dims
    chunks = BASE // rows
    groups = n_ctx // GROUP
    width = dy.shape[-1]
    top = levels - 1

    dp = lax.axis_index("dp")
    me = lax.axis_index("ctx")
    q = lax.div(me, GROUP)
    r = lax.rem(me, GROUP)
    half = lax.div(r, 2)
    core = lax.rem(r, 2)
    outer = half == core
    sibling = me + 1 - 2 * core
    partner = me + 2 - 4 * half
    has_next = q < groups - 1
    has_prev = q > 0
    lower = half == 0
    z_sends = jnp.logical_or(jnp.logical_and(lower, has_next), jnp.logical_and(half == 1, has_prev))
    z_recvs = jnp.logical_or(jnp.logical_and(lower, has_prev), jnp.logical_and(half == 1, has_next))

    own_load = pltpu.make_async_copy(cot, dy.at[2], load_sem.at[0])
    in_loads = [
        pltpu.make_async_copy(first, inputs.at[0], load_sem.at[1]),
        pltpu.make_async_copy(fwd, inputs.at[pl.ds(1, top)], load_sem.at[2]),
        pltpu.make_async_copy(rev, inputs.at[pl.ds(levels, top)], load_sem.at[3]),
    ]
    small_loads = [
        pltpu.make_async_copy(filt_in, filt, load_sem.at[4]),
        pltpu.make_async_copy(mix_in, mix, load_sem.at[5]),
    ]
    for load in small_loads + [own_load] + in_loads:
        load.start()

    barrier = pltpu.get_barrier_semaphore()
    team = [(a, b) for a in range(n_dp) for b in range(GROUP) if (a, b) != (0, 0)]

    def team_member(a, b):
        return lax.rem(dp + a, n_dp), lax.rem(r + b, GROUP)

    for a, b in team:
        to_dp, to_r = team_member(a, b)
        pl.semaphore_signal(barrier, inc=1, device_id=(to_dp, q * GROUP + to_r), device_id_type=MESH)
    for k in range(1, groups):
        to_q = lax.rem(q + k, groups)
        pl.semaphore_signal(barrier, inc=1, device_id=(dp, to_q * GROUP + r), device_id_type=MESH)
    pl.semaphore_wait(barrier, len(team) + groups - 1)

    def part(ref, c):
        return ref.at[:, pl.ds(pl.multiple_of(c * rows, rows), rows), :]

    def hop(kind, c):
        if kind == 0:
            src, slot, to = part(cot, c), 4 * half, partner
        elif kind == 1:
            src, slot, to = part(cot, c), 1 + 2 * core, sibling
        elif kind == 2:
            src, slot, to = part(dy.at[4 - 4 * half], c), 4 * half, me + 4 - 8 * half
        else:
            src, slot, to = part(dy.at[4 - 4 * core], c), 3 - 2 * core, sibling
        return pltpu.make_async_remote_copy(
            src_ref=src,
            dst_ref=part(dy.at[slot], c),
            send_sem=send_sem.at[kind, c],
            recv_sem=recv_sem.at[kind, c],
            device_id=(dp, to),
            device_id_type=MESH,
        )

    @pl.loop(0, chunks)
    def _(c):
        hop(0, c).start()
        hop(1, c).start()

    @pl.when(jnp.logical_not(z_recvs))
    def _():
        dy[4 * half] = jnp.zeros(dy.shape[1:], dy.dtype)

    @pl.when(jnp.logical_and(jnp.logical_not(z_recvs), outer))
    def _():
        dy[1 + 2 * core] = jnp.zeros(dy.shape[1:], dy.dtype)

    for load in small_loads:
        load.wait()

    def weight(b, level):
        return mix[level, b : b + 1, :]

    for b in range(2):
        f00, f01 = filt[b, 0, 0:1, :], filt[b, 0, 1:2, :]
        f10, f11 = filt[b, 1, 0:1, :], filt[b, 1, 1:2, :]
        last, w = weight(b, levels), weight(b, top)
        values = [f01, f00, f01 * last + f11 * w, f00 * last + f10 * w]
        for level in range(top):
            w = weight(b, level)
            values += [f11 * w, f10 * w]
        for k, value in enumerate(values):
            coef[b, k : k + 1, :] = value
    sums[...] = jnp.zeros(sums.shape, F32)
    plain_sums[...] = jnp.zeros(plain_sums.shape, F32)

    n_sums = 1 + 3 * top
    lane_blocks = width // LANES

    def window(row, lane):
        return (
            pl.ds(pl.multiple_of(row, STRIP), STRIP),
            pl.ds(pl.multiple_of(lane, LANES), LANES),
        )

    def pieces(first_row, n_rows, work):
        @pl.loop(0, (n_rows // STRIP) * lane_blocks)
        def _(piece):
            row = first_row + lax.div(piece, lane_blocks) * STRIP
            work(*window(row, lax.rem(piece, lane_blocks) * LANES))

    def prepare(rows_at, lanes_at):
        own = []
        for j in range(units):
            own.append(dy[2, j, rows_at, lanes_at].astype(F32))
            dy_wide[j, rows_at, lanes_at] = own[j]
        for slot in range(2 * levels - 1):
            t_y = None
            for j in range(units):
                p = inputs[slot, j, rows_at, lanes_at].astype(F32)
                inputs_wide[slot, j, rows_at, lanes_at] = p
                t_y = own[j] * p if t_y is None else t_y + own[j] * p
            plain_sums[slot, :, lanes_at] += t_y

    def branch(b, last, rows_at, lanes_at):
        sign = 1 - 2 * b

        def place(m):
            return b * (units - 1) + sign * (m % units)

        for m in range(units, units + 2**levels - 1):
            strip = dy[2 + sign * (m // units), place(m), rows_at, lanes_at]
            halo[m - units] = strip.astype(F32)

        def dy_at(m):
            return dy_wide[place(m), rows_at, lanes_at] if m < units else halo[m - units]

        def input_at(level, m):
            slot = 0 if level == 0 else level + top * b
            return inputs_wide[slot, place(m), rows_at, lanes_at]

        def factor_at(k):
            return coef[b, k : k + 1, lanes_at]

        def add(k, value):
            sums[b * n_sums + k, :, lanes_at] += value

        shift = 2**top
        y = [dy_at(m) for m in range(units + 2 * shift - 1)]
        s_y = None
        for m in range(units):
            s = y[m + shift] * input_at(top, m)
            s_y = s if s_y is None else s_y + s
        add(0, s_y)
        here, there = factor_at(2), factor_at(3)
        g = [here * y[m] + there * y[m + shift] for m in range(units + shift - 1)]
        for level in reversed(range(top)):
            shift = 2**level
            y = [dy_at(m) for m in range(units + 2 * shift - 1)]
            acc = None
            for m in range(units):
                p = input_at(level, m)
                terms = [g[m + shift] * p, y[m + shift] * p, g[m] * p]
                acc = terms if acc is None else [u + v for u, v in zip(acc, terms)]
            for k in range(3):
                add(1 + 3 * level + k, acc[k])
            f01, f00 = factor_at(0), factor_at(1)
            w1, w0 = factor_at(4 + 2 * level), factor_at(5 + 2 * level)
            g = [
                f01 * g[m] + w1 * y[m] + (f00 * g[m + shift] + w0 * y[m + shift])
                for m in range(units + shift - 1)
            ]
        for m in range(units):
            if last:
                total = partial[place(m), rows_at, lanes_at] + g[m]
                out[place(m), rows_at, lanes_at] = total.astype(out.dtype)
            else:
                partial[place(m), rows_at, lanes_at] = g[m]

    own_load.wait()
    for load in in_loads:
        load.wait()
    pieces(0, BASE, prepare)

    soon, mid, late = 1, 2, 3

    @pl.loop(0, chunks + late)
    def _(step):
        @pl.when(step < chunks)
        def _():
            hop(0, step).wait_recv()

            @pl.when(z_sends)
            def _():
                hop(2, step).start()

            @pl.when(outer)
            def _():
                hop(3, step).start()

        @pl.when(jnp.logical_and(step >= mid, step < chunks + mid))
        def _():
            c = step - mid

            @pl.when(z_recvs)
            def _():
                hop(2, c).wait_recv()

                @pl.when(jnp.logical_not(outer))
                def _():
                    hop(3, c).start()

        @pl.when(jnp.logical_and(step >= soon, step < chunks + soon))
        def _():
            c = step - soon
            hop(1, c).wait_recv()

            @pl.when(jnp.logical_not(outer))
            def _():
                hop(3, c).wait_recv()

            pieces(c * rows, rows, functools.partial(branch, half, False))

        @pl.when(step >= late)
        def _():
            c = step - late

            @pl.when(jnp.logical_and(outer, z_recvs))
            def _():
                hop(3, c).wait_recv()

            pieces(c * rows, rows, functools.partial(branch, 1 - half, True))

    slot_a = dp * GROUP + r
    n_filt = 8
    for b in range(2):
        f00, f01 = filt[b, 0, 0:1, :], filt[b, 0, 1:2, :]
        f10, f11 = filt[b, 1, 0:1, :], filt[b, 1, 1:2, :]

        def total(k):
            return jnp.sum(sums[b * n_sums + k], axis=0, keepdims=True)

        def plain_total(level):
            slot = 0 if level == 0 else level + top * b
            return jnp.sum(plain_sums[slot], axis=0, keepdims=True)

        def put(k, value):
            buf_a[slot_a, k : k + 1, :] = value

        s_y, t_y = total(0), plain_total(top)
        last, w = weight(b, levels), weight(b, top)
        terms = [last * s_y, last * t_y, w * s_y, w * t_y]
        base = n_filt + b * (levels + 1)
        put(base + levels, f00 * s_y + f01 * t_y)
        put(base + top, f10 * s_y + f11 * t_y)
        for level in reversed(range(top)):
            s_a, s_y, t_a = [total(1 + 3 * level + k) for k in range(3)]
            t_y = plain_total(level)
            w = weight(b, level)
            terms = [u + v for u, v in zip(terms, [s_a, t_a, w * s_y, w * t_y])]
            put(base + level, f10 * s_y + f11 * t_y)
        for k in range(4):
            put(4 * b + k, terms[k])

    def team_copy(a, b):
        to_dp, to_r = team_member(a, b)
        slot = dp * GROUP + r
        return pltpu.make_async_remote_copy(
            src_ref=buf_a.at[slot],
            dst_ref=buf_a.at[slot],
            send_sem=send_a.at[a * GROUP + b],
            recv_sem=recv_a.at[a * GROUP + b],
            device_id=(to_dp, q * GROUP + to_r),
            device_id_type=MESH,
        )

    def group_copy(k):
        to_q = lax.rem(q + k, groups)
        return pltpu.make_async_remote_copy(
            src_ref=buf_b.at[q],
            dst_ref=buf_b.at[q],
            send_sem=send_b.at[k],
            recv_sem=recv_b.at[k],
            device_id=(dp, to_q * GROUP + r),
            device_id_type=MESH,
        )

    for a, b in team:
        team_copy(a, b).start()
    for a, b in team:
        team_copy(a, b).wait_recv()
    value = buf_a[0]
    for k in range(1, n_dp * GROUP):
        value = value + buf_a[k]
    buf_b[q] = value
    for k in range(1, groups):
        group_copy(k).start()
    for k in range(1, groups):
        group_copy(k).wait_recv()
    value = buf_b[0]
    for k in range(1, groups):
        value = value + buf_b[k]
    value = value * factor
    for b in range(2):
        for kind in range(2):
            at = 4 * b + 2 * kind
            out_filt[b, kind] = value[at : at + 2]
        base = n_filt + b * (levels + 1)
        out_mix[:, b] = value[base : base + levels + 1]

    for a, b in team:
        team_copy(a, b).wait_send()
    for k in range(1, groups):
        group_copy(k).wait_send()

    @pl.loop(0, chunks)
    def _(c):
        hop(0, c).wait_send()
        hop(1, c).wait_send()

        @pl.when(z_sends)
        def _():
            hop(2, c).wait_send()

        @pl.when(jnp.logical_or(outer, z_recvs))
        def _():
            hop(3, c).wait_send()


def body(level_input, saved_forward, saved_reverse, filters, mixing, cotangent):
    n_dp, n_ctx = lax.axis_size("dp"), lax.axis_size("ctx")
    levels = saved_forward.shape[0] + 1
    seqs, span, width = level_input.shape
    units = span // BASE
    assert seqs == 1 and span % BASE == 0 and n_ctx % GROUP == 0
    assert 2**levels <= 2 * units and width % LANES == 0
    rows = STRIP
    chunks = BASE // rows
    top = levels - 1
    groups = n_ctx // GROUP
    factor = 1.0 / math.sqrt(seqs * n_dp * span * n_ctx)
    terms = 8 + 2 * (levels + 1)
    block = (units, BASE, width)
    by_level = mixing.transpose(1, 0, 2)
    dma = pltpu.SemaphoreType.DMA
    hbm = pl.BlockSpec(memory_space=pltpu.HBM)
    vmem = pl.BlockSpec(memory_space=pltpu.VMEM)
    grad_input, grad_filters, grad_mixing = pl.pallas_call(
        functools.partial(kernel, (n_dp, n_ctx, units, levels, rows, factor)),
        out_shape=(
            pltpu.VMEM(block, jnp.bfloat16),
            pltpu.VMEM(filters.shape, F32),
            pltpu.VMEM(by_level.shape, F32),
        ),
        in_specs=[hbm] * 6,
        out_specs=(vmem, vmem, vmem),
        scratch_shapes=[
            pltpu.VMEM((5,) + block, jnp.bfloat16),
            pltpu.VMEM((2 * levels - 1,) + block, jnp.bfloat16),
            pltpu.VMEM(filters.shape, F32),
            pltpu.VMEM(by_level.shape, F32),
            pltpu.VMEM(block, F32),
            pltpu.VMEM((2 * levels - 1,) + block, F32),
            pltpu.VMEM((2**levels - 1, STRIP, LANES), F32),
            pltpu.VMEM(block, F32),
            pltpu.VMEM((2 * levels - 1, STRIP, width), F32),
            pltpu.VMEM((2 * (1 + 3 * top), STRIP, width), F32),
            pltpu.VMEM((2, 4 + 2 * top, width), F32),
            pltpu.VMEM((n_dp * GROUP, terms, width), F32),
            pltpu.VMEM((groups, terms, width), F32),
            dma((6,)),
            dma((4, chunks)),
            dma((4, chunks)),
            dma((n_dp * GROUP,)),
            dma((n_dp * GROUP,)),
            dma((groups,)),
            dma((groups,)),
        ],
        compiler_params=pltpu.CompilerParams(
            collective_id=0, has_side_effects=True, vmem_limit_bytes=32 * 1024 * 1024
        ),
        cost_estimate=pl.CostEstimate(
            flops=300 * span * width, bytes_accessed=9 * span * width * 2, transcendentals=0
        ),
    )(
        *[
            pltpu.with_memory_space_constraint(operand, pltpu.HBM)
            for operand in (
                cotangent.reshape(block),
                level_input.reshape(block),
                saved_forward.reshape((top,) + block),
                saved_reverse.reshape((top,) + block),
                filters,
                by_level,
            )
        ]
    )
    return (grad_input.reshape(level_input.shape), grad_filters, grad_mixing.transpose(1, 0, 2))


def solution(mesh):
    return jax.shard_map(
        body,
        mesh=mesh,
        in_specs=(
            P("dp", "ctx", None),
            P(None, "dp", "ctx", None),
            P(None, "dp", "ctx", None),
            P(),
            P(),
            P("dp", "ctx", None),
        ),
        out_specs=(P("dp", "ctx", None), P(), P()),
        check_vma=False,
    )
```

```python
import functools
import math

import jax
import jax.numpy as jnp
from jax import lax
from jax.experimental import pallas as pl
from jax.experimental.pallas import tpu as pltpu
from jax.sharding import PartitionSpec as P

BASE = 128
STRIP = 16
LANES = 128
GROUP = 4
HALVES = 2
AHEAD = 3
MESH = pl.DeviceIdType.MESH
F32 = jnp.float32


def kernel(
    dims,
    cot,
    first,
    fwd,
    rev,
    filt_in,
    mix_in,
    out,
    out_filt,
    out_mix,
    dy,
    inputs,
    filt,
    mix,
    dy_wide,
    inputs_wide,
    halo,
    partial,
    plain_sums,
    sums,
    coef,
    buf_a,
    buf_b,
    load_sem,
    send_sem,
    recv_sem,
    send_a,
    recv_a,
    send_b,
    recv_b,
):
    n_dp, n_ctx, units, levels, rows, factor = dims
    chunks = BASE // rows
    groups = n_ctx // GROUP
    width = dy.shape[-1]
    top = levels - 1

    dp = lax.axis_index("dp")
    me = lax.axis_index("ctx")
    q = lax.div(me, GROUP)
    r = lax.rem(me, GROUP)
    half = lax.div(r, 2)
    core = lax.rem(r, 2)
    outer = half == core
    sibling = me + 1 - 2 * core
    partner = me + 2 - 4 * half
    has_next = q < groups - 1
    has_prev = q > 0
    lower = half == 0
    z_sends = jnp.logical_or(jnp.logical_and(lower, has_next), jnp.logical_and(half == 1, has_prev))
    z_recvs = jnp.logical_or(jnp.logical_and(lower, has_prev), jnp.logical_and(half == 1, has_next))

    own_load = pltpu.make_async_copy(cot, dy.at[2], load_sem.at[0])
    in_loads = [
        pltpu.make_async_copy(first, inputs.at[0], load_sem.at[1]),
        pltpu.make_async_copy(fwd, inputs.at[pl.ds(1, top)], load_sem.at[2]),
        pltpu.make_async_copy(rev, inputs.at[pl.ds(levels, top)], load_sem.at[3]),
    ]
    small_loads = [
        pltpu.make_async_copy(filt_in, filt, load_sem.at[4]),
        pltpu.make_async_copy(mix_in, mix, load_sem.at[5]),
    ]
    for load in small_loads + [own_load] + in_loads:
        load.start()

    barrier = pltpu.get_barrier_semaphore()
    team = [(a, b) for a in range(n_dp) for b in range(GROUP) if (a, b) != (0, 0)]

    def team_member(a, b):
        return lax.rem(dp + a, n_dp), lax.rem(r + b, GROUP)

    for a, b in team:
        to_dp, to_r = team_member(a, b)
        pl.semaphore_signal(barrier, inc=1, device_id=(to_dp, q * GROUP + to_r), device_id_type=MESH)
    for k in range(1, groups):
        to_q = lax.rem(q + k, groups)
        pl.semaphore_signal(barrier, inc=1, device_id=(dp, to_q * GROUP + r), device_id_type=MESH)
    pl.semaphore_wait(barrier, len(team) + groups - 1)

    def part(ref, c, h):
        some = units // HALVES
        return ref.at[pl.ds(h * some, some), pl.ds(pl.multiple_of(c * rows, rows), rows), :]

    def hop(kind, c, h):
        if kind == 0:
            src, slot, to = cot, 4 * half, partner
        elif kind == 1:
            src, slot, to = cot, 1 + 2 * core, sibling
        elif kind == 2:
            src, slot, to = dy.at[4 - 4 * half], 4 * half, me + 4 - 8 * half
        else:
            src, slot, to = dy.at[4 - 4 * core], 3 - 2 * core, sibling
        return pltpu.make_async_remote_copy(
            src_ref=part(src, c, h),
            dst_ref=part(dy.at[slot], c, h),
            send_sem=send_sem.at[kind, c, h],
            recv_sem=recv_sem.at[kind, c, h],
            device_id=(dp, to),
            device_id_type=MESH,
        )

    def send_own(c):
        for kind in range(2):
            for h in range(HALVES):
                hop(kind, c, h).start()

    ahead = min(AHEAD, chunks)
    for c in range(ahead):
        send_own(c)

    @pl.when(jnp.logical_not(z_recvs))
    def _():
        dy[4 * half] = jnp.zeros(dy.shape[1:], dy.dtype)

    @pl.when(jnp.logical_and(jnp.logical_not(z_recvs), outer))
    def _():
        dy[1 + 2 * core] = jnp.zeros(dy.shape[1:], dy.dtype)

    for load in small_loads:
        load.wait()

    def weight(b, level):
        return mix[level, b : b + 1, :]

    for b in range(2):
        f00, f01 = filt[b, 0, 0:1, :], filt[b, 0, 1:2, :]
        f10, f11 = filt[b, 1, 0:1, :], filt[b, 1, 1:2, :]
        last, w = weight(b, levels), weight(b, top)
        values = [f01, f00, f01 * last + f11 * w, f00 * last + f10 * w]
        for level in range(top):
            w = weight(b, level)
            values += [f11 * w, f10 * w]
        for k, value in enumerate(values):
            coef[b, k : k + 1, :] = value
    sums[...] = jnp.zeros(sums.shape, F32)
    plain_sums[...] = jnp.zeros(plain_sums.shape, F32)

    n_sums = 1 + 3 * top
    lane_blocks = width // LANES

    def window(row, lane):
        return (
            pl.ds(pl.multiple_of(row, STRIP), STRIP),
            pl.ds(pl.multiple_of(lane, LANES), LANES),
        )

    def pieces(first_row, n_rows, work):
        @pl.loop(0, (n_rows // STRIP) * lane_blocks)
        def _(piece):
            row = first_row + lax.div(piece, lane_blocks) * STRIP
            work(*window(row, lax.rem(piece, lane_blocks) * LANES))

    def prepare(rows_at, lanes_at):
        own = []
        for j in range(units):
            own.append(dy[2, j, rows_at, lanes_at].astype(F32))
            dy_wide[j, rows_at, lanes_at] = own[j]
        for slot in range(2 * levels - 1):
            t_y = None
            for j in range(units):
                p = inputs[slot, j, rows_at, lanes_at].astype(F32)
                inputs_wide[slot, j, rows_at, lanes_at] = p
                t_y = own[j] * p if t_y is None else t_y + own[j] * p
            plain_sums[slot, :, lanes_at] += t_y

    def branch(b, last, rows_at, lanes_at):
        sign = 1 - 2 * b

        def place(m):
            return b * (units - 1) + sign * (m % units)

        for m in range(units, units + 2**levels - 1):
            strip = dy[2 + sign * (m // units), place(m), rows_at, lanes_at]
            halo[m - units] = strip.astype(F32)

        def dy_at(m):
            return dy_wide[place(m), rows_at, lanes_at] if m < units else halo[m - units]

        def input_at(level, m):
            slot = 0 if level == 0 else level + top * b
            return inputs_wide[slot, place(m), rows_at, lanes_at]

        def factor_at(k):
            return coef[b, k : k + 1, lanes_at]

        def add(k, value):
            sums[b * n_sums + k, :, lanes_at] += value

        shift = 2**top
        y = [dy_at(m) for m in range(units + 2 * shift - 1)]
        s_y = None
        for m in range(units):
            s = y[m + shift] * input_at(top, m)
            s_y = s if s_y is None else s_y + s
        add(0, s_y)
        here, there = factor_at(2), factor_at(3)
        g = [here * y[m] + there * y[m + shift] for m in range(units + shift - 1)]
        for level in reversed(range(top)):
            shift = 2**level
            y = [dy_at(m) for m in range(units + 2 * shift - 1)]
            acc = None
            for m in range(units):
                p = input_at(level, m)
                terms = [g[m + shift] * p, y[m + shift] * p, g[m] * p]
                acc = terms if acc is None else [u + v for u, v in zip(acc, terms)]
            for k in range(3):
                add(1 + 3 * level + k, acc[k])
            f01, f00 = factor_at(0), factor_at(1)
            w1, w0 = factor_at(4 + 2 * level), factor_at(5 + 2 * level)
            g = [
                f01 * g[m] + w1 * y[m] + (f00 * g[m + shift] + w0 * y[m + shift])
                for m in range(units + shift - 1)
            ]
        for m in range(units):
            if last:
                total = partial[place(m), rows_at, lanes_at] + g[m]
                out[place(m), rows_at, lanes_at] = total.astype(out.dtype)
            else:
                partial[place(m), rows_at, lanes_at] = g[m]

    own_load.wait()
    for load in in_loads:
        load.wait()
    pieces(0, BASE, prepare)

    soon, mid, late = 1, 2, 3

    @pl.loop(0, chunks + late)
    def _(step):
        @pl.when(step < chunks)
        def _():
            for h in range(HALVES):
                hop(0, step, h).wait_recv()

                @pl.when(z_sends)
                def _():
                    hop(2, step, h).start()

                @pl.when(outer)
                def _():
                    hop(3, step, h).start()

            @pl.when(step + ahead < chunks)
            def _():
                send_own(step + ahead)

        @pl.when(jnp.logical_and(step >= mid, step < chunks + mid))
        def _():
            c = step - mid

            @pl.when(z_recvs)
            def _():
                for h in range(HALVES):
                    hop(2, c, h).wait_recv()

                    @pl.when(jnp.logical_not(outer))
                    def _():
                        hop(3, c, h).start()

        @pl.when(jnp.logical_and(step >= soon, step < chunks + soon))
        def _():
            c = step - soon
            for h in range(HALVES):
                hop(1, c, h).wait_recv()

            @pl.when(jnp.logical_not(outer))
            def _():
                for h in range(HALVES):
                    hop(3, c, h).wait_recv()

            pieces(c * rows, rows, functools.partial(branch, half, False))

        @pl.when(step >= late)
        def _():
            c = step - late

            @pl.when(jnp.logical_and(outer, z_recvs))
            def _():
                for h in range(HALVES):
                    hop(3, c, h).wait_recv()

            pieces(c * rows, rows, functools.partial(branch, 1 - half, True))

    slot_a = dp * GROUP + r
    n_filt = 8
    for b in range(2):
        f00, f01 = filt[b, 0, 0:1, :], filt[b, 0, 1:2, :]
        f10, f11 = filt[b, 1, 0:1, :], filt[b, 1, 1:2, :]

        def total(k):
            return jnp.sum(sums[b * n_sums + k], axis=0, keepdims=True)

        def plain_total(level):
            slot = 0 if level == 0 else level + top * b
            return jnp.sum(plain_sums[slot], axis=0, keepdims=True)

        def put(k, value):
            buf_a[slot_a, k : k + 1, :] = value

        s_y, t_y = total(0), plain_total(top)
        last, w = weight(b, levels), weight(b, top)
        terms = [last * s_y, last * t_y, w * s_y, w * t_y]
        base = n_filt + b * (levels + 1)
        put(base + levels, f00 * s_y + f01 * t_y)
        put(base + top, f10 * s_y + f11 * t_y)
        for level in reversed(range(top)):
            s_a, s_y, t_a = [total(1 + 3 * level + k) for k in range(3)]
            t_y = plain_total(level)
            w = weight(b, level)
            terms = [u + v for u, v in zip(terms, [s_a, t_a, w * s_y, w * t_y])]
            put(base + level, f10 * s_y + f11 * t_y)
        for k in range(4):
            put(4 * b + k, terms[k])

    def team_copy(a, b):
        to_dp, to_r = team_member(a, b)
        slot = dp * GROUP + r
        return pltpu.make_async_remote_copy(
            src_ref=buf_a.at[slot],
            dst_ref=buf_a.at[slot],
            send_sem=send_a.at[a * GROUP + b],
            recv_sem=recv_a.at[a * GROUP + b],
            device_id=(to_dp, q * GROUP + to_r),
            device_id_type=MESH,
        )

    def group_copy(k):
        to_q = lax.rem(q + k, groups)
        return pltpu.make_async_remote_copy(
            src_ref=buf_b.at[q],
            dst_ref=buf_b.at[q],
            send_sem=send_b.at[k],
            recv_sem=recv_b.at[k],
            device_id=(dp, to_q * GROUP + r),
            device_id_type=MESH,
        )

    for a, b in team:
        team_copy(a, b).start()

    @pl.loop(0, chunks)
    def _(c):
        for h in range(HALVES):
            hop(0, c, h).wait_send()
            hop(1, c, h).wait_send()

            @pl.when(z_sends)
            def _():
                hop(2, c, h).wait_send()

            @pl.when(jnp.logical_or(outer, z_recvs))
            def _():
                hop(3, c, h).wait_send()

    for a, b in team:
        team_copy(a, b).wait_recv()
    value = buf_a[0]
    for k in range(1, n_dp * GROUP):
        value = value + buf_a[k]
    buf_b[q] = value
    for k in range(1, groups):
        group_copy(k).start()
    for k in range(1, groups):
        group_copy(k).wait_recv()
    value = buf_b[0]
    for k in range(1, groups):
        value = value + buf_b[k]
    value = value * factor
    for b in range(2):
        for kind in range(2):
            at = 4 * b + 2 * kind
            out_filt[b, kind] = value[at : at + 2]
        base = n_filt + b * (levels + 1)
        out_mix[:, b] = value[base : base + levels + 1]

    for a, b in team:
        team_copy(a, b).wait_send()
    for k in range(1, groups):
        group_copy(k).wait_send()


def hand_over(*refs):
    sources, targets, sem = refs[:3], refs[3:6], refs[6]
    copies = [pltpu.make_async_copy(sources[k], targets[k], sem.at[k]) for k in range(3)]
    for copy in copies:
        copy.start()
    for copy in copies:
        copy.wait()


def body(level_input, saved_forward, saved_reverse, filters, mixing, cotangent):
    n_dp, n_ctx = lax.axis_size("dp"), lax.axis_size("ctx")
    levels = saved_forward.shape[0] + 1
    seqs, span, width = level_input.shape
    units = span // BASE
    assert seqs == 1 and span % BASE == 0 and n_ctx % GROUP == 0
    assert units % HALVES == 0
    assert 2**levels <= 2 * units and width % LANES == 0
    rows = STRIP
    chunks = BASE // rows
    top = levels - 1
    groups = n_ctx // GROUP
    factor = 1.0 / math.sqrt(seqs * n_dp * span * n_ctx)
    terms = 8 + 2 * (levels + 1)
    block = (units, BASE, width)
    by_level = mixing.transpose(1, 0, 2)
    dma = pltpu.SemaphoreType.DMA
    hbm = pl.BlockSpec(memory_space=pltpu.HBM)
    vmem = pl.BlockSpec(memory_space=pltpu.VMEM)
    grad_input, grad_filters, grad_mixing = pl.pallas_call(
        functools.partial(kernel, (n_dp, n_ctx, units, levels, rows, factor)),
        out_shape=(
            pltpu.VMEM(block, jnp.bfloat16),
            pltpu.VMEM(filters.shape, F32),
            pltpu.VMEM(by_level.shape, F32),
        ),
        in_specs=[hbm] * 6,
        out_specs=(vmem, vmem, vmem),
        scratch_shapes=[
            pltpu.VMEM((5,) + block, jnp.bfloat16),
            pltpu.VMEM((2 * levels - 1,) + block, jnp.bfloat16),
            pltpu.VMEM(filters.shape, F32),
            pltpu.VMEM(by_level.shape, F32),
            pltpu.VMEM(block, F32),
            pltpu.VMEM((2 * levels - 1,) + block, F32),
            pltpu.VMEM((2**levels - 1, STRIP, LANES), F32),
            pltpu.VMEM(block, F32),
            pltpu.VMEM((2 * levels - 1, STRIP, width), F32),
            pltpu.VMEM((2 * (1 + 3 * top), STRIP, width), F32),
            pltpu.VMEM((2, 4 + 2 * top, width), F32),
            pltpu.VMEM((n_dp * GROUP, terms, width), F32),
            pltpu.VMEM((groups, terms, width), F32),
            dma((6,)),
            dma((4, chunks, HALVES)),
            dma((4, chunks, HALVES)),
            dma((n_dp * GROUP,)),
            dma((n_dp * GROUP,)),
            dma((groups,)),
            dma((groups,)),
        ],
        compiler_params=pltpu.CompilerParams(
            collective_id=0, has_side_effects=True, vmem_limit_bytes=32 * 1024 * 1024
        ),
        cost_estimate=pl.CostEstimate(
            flops=300 * span * width, bytes_accessed=9 * span * width * 2, transcendentals=0
        ),
    )(
        *[
            pltpu.with_memory_space_constraint(operand, pltpu.HBM)
            for operand in (
                cotangent.reshape(block),
                level_input.reshape(block),
                saved_forward.reshape((top,) + block),
                saved_reverse.reshape((top,) + block),
                filters,
                by_level,
            )
        ]
    )
    results = (grad_input, grad_filters, grad_mixing)
    grad_input, grad_filters, grad_mixing = pl.pallas_call(
        hand_over,
        out_shape=tuple(pltpu.HBM(x.shape, x.dtype) for x in results),
        in_specs=[vmem] * 3,
        out_specs=(hbm,) * 3,
        scratch_shapes=[dma((3,))],
        cost_estimate=pl.CostEstimate(flops=0, bytes_accessed=2 * span * width * 2, transcendentals=0),
    )(*[pltpu.with_memory_space_constraint(x, pltpu.VMEM) for x in results])
    return (grad_input.reshape(level_input.shape), grad_filters, grad_mixing.transpose(1, 0, 2))


def solution(mesh):
    return jax.shard_map(
        body,
        mesh=mesh,
        in_specs=(
            P("dp", "ctx", None),
            P(None, "dp", "ctx", None),
            P(None, "dp", "ctx", None),
            P(),
            P(),
            P("dp", "ctx", None),
        ),
        out_specs=(P("dp", "ctx", None), P(), P()),
        check_vma=False,
    )
```

```python
import functools
import math

import jax
import jax.numpy as jnp
from jax import lax
from jax.experimental import pallas as pl
from jax.experimental.pallas import tpu as pltpu
from jax.sharding import PartitionSpec as P

BASE = 128
STRIP = 16
TILE = 8
LANES = 128
GROUP = 4
HALVES = 2
AHEAD = 3
MESH = pl.DeviceIdType.MESH
F32 = jnp.float32


def kernel(
    dims,
    cot,
    first,
    fwd,
    rev,
    filt_in,
    mix_in,
    out,
    out_filt,
    out_mix,
    dy,
    inputs,
    filt,
    mix,
    dy_wide,
    inputs_wide,
    halo,
    partial,
    plain_sums,
    sums,
    coef,
    buf_a,
    buf_b,
    load_sem,
    send_sem,
    recv_sem,
    send_a,
    recv_a,
    send_b,
    recv_b,
):
    n_dp, n_ctx, units, levels, rows, factor = dims
    chunks = BASE // rows
    groups = n_ctx // GROUP
    width = dy.shape[-1]
    top = levels - 1

    dp = lax.axis_index("dp")
    me = lax.axis_index("ctx")
    q = lax.div(me, GROUP)
    r = lax.rem(me, GROUP)
    half = lax.div(r, 2)
    core = lax.rem(r, 2)
    outer = half == core
    sibling = me + 1 - 2 * core
    partner = me + 2 - 4 * half
    has_next = q < groups - 1
    has_prev = q > 0
    lower = half == 0
    z_sends = jnp.logical_or(jnp.logical_and(lower, has_next), jnp.logical_and(half == 1, has_prev))
    z_recvs = jnp.logical_or(jnp.logical_and(lower, has_prev), jnp.logical_and(half == 1, has_next))

    own_load = pltpu.make_async_copy(cot, dy.at[2], load_sem.at[0])
    in_loads = [
        pltpu.make_async_copy(first, inputs.at[0], load_sem.at[1]),
        pltpu.make_async_copy(fwd, inputs.at[pl.ds(1, top)], load_sem.at[2]),
        pltpu.make_async_copy(rev, inputs.at[pl.ds(levels, top)], load_sem.at[3]),
    ]
    small_loads = [
        pltpu.make_async_copy(filt_in, filt, load_sem.at[4]),
        pltpu.make_async_copy(mix_in, mix, load_sem.at[5]),
    ]
    for load in small_loads + [own_load] + in_loads:
        load.start()

    barrier = pltpu.get_barrier_semaphore()
    team = [(a, b) for a in range(n_dp) for b in range(GROUP) if (a, b) != (0, 0)]

    def team_member(a, b):
        return lax.rem(dp + a, n_dp), lax.rem(r + b, GROUP)

    for a, b in team:
        to_dp, to_r = team_member(a, b)
        pl.semaphore_signal(barrier, inc=1, device_id=(to_dp, q * GROUP + to_r), device_id_type=MESH)
    for k in range(1, groups):
        to_q = lax.rem(q + k, groups)
        pl.semaphore_signal(barrier, inc=1, device_id=(dp, to_q * GROUP + r), device_id_type=MESH)
    pl.semaphore_wait(barrier, len(team) + groups - 1)

    def part(ref, c, h):
        some = units // HALVES
        return ref.at[pl.ds(h * some, some), pl.ds(pl.multiple_of(c * rows, rows), rows), :]

    def hop(kind, c, h):
        if kind == 0:
            src, slot, to = cot, 4 * half, partner
        elif kind == 1:
            src, slot, to = cot, 1 + 2 * core, sibling
        elif kind == 2:
            src, slot, to = dy.at[4 - 4 * half], 4 * half, me + 4 - 8 * half
        else:
            src, slot, to = dy.at[4 - 4 * core], 3 - 2 * core, sibling
        return pltpu.make_async_remote_copy(
            src_ref=part(src, c, h),
            dst_ref=part(dy.at[slot], c, h),
            send_sem=send_sem.at[kind, c, h],
            recv_sem=recv_sem.at[kind, c, h],
            device_id=(dp, to),
            device_id_type=MESH,
        )

    def send_own(c):
        for kind in range(2):
            for h in range(HALVES):
                hop(kind, c, h).start()

    ahead = min(AHEAD, chunks)
    for c in range(ahead):
        send_own(c)

    @pl.when(jnp.logical_not(z_recvs))
    def _():
        dy[4 * half] = jnp.zeros(dy.shape[1:], dy.dtype)

    @pl.when(jnp.logical_and(jnp.logical_not(z_recvs), outer))
    def _():
        dy[1 + 2 * core] = jnp.zeros(dy.shape[1:], dy.dtype)

    for load in small_loads:
        load.wait()

    def weight(b, level):
        return mix[level, b : b + 1, :]

    for b in range(2):
        f00, f01 = filt[b, 0, 0:1, :], filt[b, 0, 1:2, :]
        f10, f11 = filt[b, 1, 0:1, :], filt[b, 1, 1:2, :]
        last, w = weight(b, levels), weight(b, top)
        values = [f01, f00, f01 * last + f11 * w, f00 * last + f10 * w]
        for level in range(top):
            w = weight(b, level)
            values += [f11 * w, f10 * w]
        for k, value in enumerate(values):
            coef[b, k] = jnp.broadcast_to(value, coef.shape[2:])
    sums[...] = jnp.zeros(sums.shape, F32)
    plain_sums[...] = jnp.zeros(plain_sums.shape, F32)

    n_sums = 1 + 3 * top
    lane_blocks = width // LANES

    def pieces(first_row, n_rows, size, work):
        @pl.loop(0, (n_rows // size) * lane_blocks)
        def _(piece):
            row = pl.multiple_of(lax.div(piece, lane_blocks) * size, size)
            lane = pl.multiple_of(lax.rem(piece, lane_blocks) * LANES, LANES)
            at = pl.ds(pl.multiple_of(first_row + row, size), size)
            work(at, pl.ds(row, size), pl.ds(lane, LANES))

    def prepare(rows_at, _, lanes_at):
        own = []
        for j in range(units):
            own.append(dy[2, j, rows_at, lanes_at].astype(F32))
            dy_wide[j, rows_at, lanes_at] = own[j]
        for slot in range(2 * levels - 1):
            t_y = None
            for j in range(units):
                p = inputs[slot, j, rows_at, lanes_at].astype(F32)
                inputs_wide[slot, j, rows_at, lanes_at] = p
                t_y = own[j] * p if t_y is None else t_y + own[j] * p
            plain_sums[slot, :, lanes_at] += t_y[:TILE] + t_y[TILE:]

    def place(b, m):
        return b * (units - 1) + (1 - 2 * b) * (m % units)

    def widen(b, rows_at, in_chunk, lanes_at):
        for m in range(units, units + 2**levels - 1):
            strip = dy[2 + (1 - 2 * b) * (m // units), place(b, m), rows_at, lanes_at]
            halo[m - units, in_chunk, lanes_at] = strip.astype(F32)

    def branch(b, last, rows_at, in_chunk, lanes_at):
        def dy_at(m):
            if m < units:
                return dy_wide[place(b, m), rows_at, lanes_at]
            return halo[m - units, in_chunk, lanes_at]

        def input_at(level, m):
            slot = 0 if level == 0 else level + top * b
            return inputs_wide[slot, place(b, m), rows_at, lanes_at]

        def factor_at(k):
            return coef[b, k, :, lanes_at]

        def add(k, value):
            sums[b * n_sums + k, :, lanes_at] += value

        shift = 2**top
        y = [dy_at(m) for m in range(units + 2 * shift - 1)]
        s_y = None
        for m in range(units):
            s = y[m + shift] * input_at(top, m)
            s_y = s if s_y is None else s_y + s
        add(0, s_y)
        here, there = factor_at(2), factor_at(3)
        g = [here * y[m] + there * y[m + shift] for m in range(units + shift - 1)]
        for level in reversed(range(top)):
            shift = 2**level
            y = [dy_at(m) for m in range(units + 2 * shift - 1)]
            acc = None
            for m in range(units):
                p = input_at(level, m)
                terms = [g[m + shift] * p, y[m + shift] * p, g[m] * p]
                acc = terms if acc is None else [u + v for u, v in zip(acc, terms)]
            for k in range(3):
                add(1 + 3 * level + k, acc[k])
            f01, f00 = factor_at(0), factor_at(1)
            w1, w0 = factor_at(4 + 2 * level), factor_at(5 + 2 * level)
            g = [
                f01 * g[m] + w1 * y[m] + (f00 * g[m + shift] + w0 * y[m + shift])
                for m in range(units + shift - 1)
            ]
        for m in range(units):
            total = partial[place(b, m), rows_at, lanes_at] + g[m] if last else g[m]
            partial[place(b, m), rows_at, lanes_at] = total

    def finish(rows_at, _, lanes_at):
        for j in range(units):
            out[j, rows_at, lanes_at] = partial[j, rows_at, lanes_at].astype(out.dtype)

    own_load.wait()
    for load in in_loads:
        load.wait()
    pieces(0, BASE, STRIP, prepare)

    soon, mid, late = 1, 2, 3

    @pl.loop(0, chunks + late)
    def _(step):
        @pl.when(step < chunks)
        def _():
            for h in range(HALVES):
                hop(0, step, h).wait_recv()

                @pl.when(z_sends)
                def _():
                    hop(2, step, h).start()

                @pl.when(outer)
                def _():
                    hop(3, step, h).start()

            @pl.when(step + ahead < chunks)
            def _():
                send_own(step + ahead)

        @pl.when(jnp.logical_and(step >= mid, step < chunks + mid))
        def _():
            c = step - mid

            @pl.when(z_recvs)
            def _():
                for h in range(HALVES):
                    hop(2, c, h).wait_recv()

                    @pl.when(jnp.logical_not(outer))
                    def _():
                        hop(3, c, h).start()

        @pl.when(jnp.logical_and(step >= soon, step < chunks + soon))
        def _():
            c = step - soon
            for h in range(HALVES):
                hop(1, c, h).wait_recv()

            @pl.when(jnp.logical_not(outer))
            def _():
                for h in range(HALVES):
                    hop(3, c, h).wait_recv()

            pieces(c * rows, rows, STRIP, functools.partial(widen, half))
            pieces(c * rows, rows, TILE, functools.partial(branch, half, False))

        @pl.when(step >= late)
        def _():
            c = step - late

            @pl.when(jnp.logical_and(outer, z_recvs))
            def _():
                for h in range(HALVES):
                    hop(3, c, h).wait_recv()

            pieces(c * rows, rows, STRIP, functools.partial(widen, 1 - half))
            pieces(c * rows, rows, TILE, functools.partial(branch, 1 - half, True))
            pieces(c * rows, rows, STRIP, finish)

    slot_a = dp * GROUP + r
    n_filt = 8
    for b in range(2):
        f00, f01 = filt[b, 0, 0:1, :], filt[b, 0, 1:2, :]
        f10, f11 = filt[b, 1, 0:1, :], filt[b, 1, 1:2, :]

        def total(k):
            return jnp.sum(sums[b * n_sums + k], axis=0, keepdims=True)

        def plain_total(level):
            slot = 0 if level == 0 else level + top * b
            return jnp.sum(plain_sums[slot], axis=0, keepdims=True)

        def put(k, value):
            buf_a[slot_a, k : k + 1, :] = value

        s_y, t_y = total(0), plain_total(top)
        last, w = weight(b, levels), weight(b, top)
        terms = [last * s_y, last * t_y, w * s_y, w * t_y]
        base = n_filt + b * (levels + 1)
        put(base + levels, f00 * s_y + f01 * t_y)
        put(base + top, f10 * s_y + f11 * t_y)
        for level in reversed(range(top)):
            s_a, s_y, t_a = [total(1 + 3 * level + k) for k in range(3)]
            t_y = plain_total(level)
            w = weight(b, level)
            terms = [u + v for u, v in zip(terms, [s_a, t_a, w * s_y, w * t_y])]
            put(base + level, f10 * s_y + f11 * t_y)
        for k in range(4):
            put(4 * b + k, terms[k])

    def team_copy(a, b):
        to_dp, to_r = team_member(a, b)
        slot = dp * GROUP + r
        return pltpu.make_async_remote_copy(
            src_ref=buf_a.at[slot],
            dst_ref=buf_a.at[slot],
            send_sem=send_a.at[a * GROUP + b],
            recv_sem=recv_a.at[a * GROUP + b],
            device_id=(to_dp, q * GROUP + to_r),
            device_id_type=MESH,
        )

    def group_copy(k):
        to_q = lax.rem(q + k, groups)
        return pltpu.make_async_remote_copy(
            src_ref=buf_b.at[q],
            dst_ref=buf_b.at[q],
            send_sem=send_b.at[k],
            recv_sem=recv_b.at[k],
            device_id=(dp, to_q * GROUP + r),
            device_id_type=MESH,
        )

    for a, b in team:
        team_copy(a, b).start()

    @pl.loop(0, chunks)
    def _(c):
        for h in range(HALVES):
            hop(0, c, h).wait_send()
            hop(1, c, h).wait_send()

            @pl.when(z_sends)
            def _():
                hop(2, c, h).wait_send()

            @pl.when(jnp.logical_or(outer, z_recvs))
            def _():
                hop(3, c, h).wait_send()

    for a, b in team:
        team_copy(a, b).wait_recv()
    value = buf_a[0]
    for k in range(1, n_dp * GROUP):
        value = value + buf_a[k]
    buf_b[q] = value
    for k in range(1, groups):
        group_copy(k).start()
    for k in range(1, groups):
        group_copy(k).wait_recv()
    value = buf_b[0]
    for k in range(1, groups):
        value = value + buf_b[k]
    value = value * factor
    for b in range(2):
        for kind in range(2):
            at = 4 * b + 2 * kind
            out_filt[b, kind] = value[at : at + 2]
        base = n_filt + b * (levels + 1)
        out_mix[:, b] = value[base : base + levels + 1]

    for a, b in team:
        team_copy(a, b).wait_send()
    for k in range(1, groups):
        group_copy(k).wait_send()


def hand_over(*refs):
    sources, targets, sem = refs[:3], refs[3:6], refs[6]
    copies = [pltpu.make_async_copy(sources[k], targets[k], sem.at[k]) for k in range(3)]
    for copy in copies:
        copy.start()
    for copy in copies:
        copy.wait()


def body(level_input, saved_forward, saved_reverse, filters, mixing, cotangent):
    n_dp, n_ctx = lax.axis_size("dp"), lax.axis_size("ctx")
    levels = saved_forward.shape[0] + 1
    seqs, span, width = level_input.shape
    units = span // BASE
    assert seqs == 1 and span % BASE == 0 and n_ctx % GROUP == 0
    assert units % HALVES == 0
    assert 2**levels <= 2 * units and width % LANES == 0
    rows = STRIP
    chunks = BASE // rows
    top = levels - 1
    groups = n_ctx // GROUP
    factor = 1.0 / math.sqrt(seqs * n_dp * span * n_ctx)
    terms = 8 + 2 * (levels + 1)
    block = (units, BASE, width)
    by_level = mixing.transpose(1, 0, 2)
    dma = pltpu.SemaphoreType.DMA
    hbm = pl.BlockSpec(memory_space=pltpu.HBM)
    vmem = pl.BlockSpec(memory_space=pltpu.VMEM)
    grad_input, grad_filters, grad_mixing = pl.pallas_call(
        functools.partial(kernel, (n_dp, n_ctx, units, levels, rows, factor)),
        out_shape=(
            pltpu.VMEM(block, jnp.bfloat16),
            pltpu.VMEM(filters.shape, F32),
            pltpu.VMEM(by_level.shape, F32),
        ),
        in_specs=[hbm] * 6,
        out_specs=(vmem, vmem, vmem),
        scratch_shapes=[
            pltpu.VMEM((5,) + block, jnp.bfloat16),
            pltpu.VMEM((2 * levels - 1,) + block, jnp.bfloat16),
            pltpu.VMEM(filters.shape, F32),
            pltpu.VMEM(by_level.shape, F32),
            pltpu.VMEM(block, F32),
            pltpu.VMEM((2 * levels - 1,) + block, F32),
            pltpu.VMEM((2**levels - 1, rows, width), F32),
            pltpu.VMEM(block, F32),
            pltpu.VMEM((2 * levels - 1, TILE, width), F32),
            pltpu.VMEM((2 * (1 + 3 * top), TILE, width), F32),
            pltpu.VMEM((2, 4 + 2 * top, TILE, width), F32),
            pltpu.VMEM((n_dp * GROUP, terms, width), F32),
            pltpu.VMEM((groups, terms, width), F32),
            dma((6,)),
            dma((4, chunks, HALVES)),
            dma((4, chunks, HALVES)),
            dma((n_dp * GROUP,)),
            dma((n_dp * GROUP,)),
            dma((groups,)),
            dma((groups,)),
        ],
        compiler_params=pltpu.CompilerParams(
            collective_id=0, has_side_effects=True, vmem_limit_bytes=32 * 1024 * 1024
        ),
        cost_estimate=pl.CostEstimate(
            flops=300 * span * width, bytes_accessed=9 * span * width * 2, transcendentals=0
        ),
    )(
        *[
            pltpu.with_memory_space_constraint(operand, pltpu.HBM)
            for operand in (
                cotangent.reshape(block),
                level_input.reshape(block),
                saved_forward.reshape((top,) + block),
                saved_reverse.reshape((top,) + block),
                filters,
                by_level,
            )
        ]
    )
    results = (grad_input, grad_filters, grad_mixing)
    grad_input, grad_filters, grad_mixing = pl.pallas_call(
        hand_over,
        out_shape=tuple(pltpu.HBM(x.shape, x.dtype) for x in results),
        in_specs=[vmem] * 3,
        out_specs=(hbm,) * 3,
        scratch_shapes=[dma((3,))],
        cost_estimate=pl.CostEstimate(flops=0, bytes_accessed=2 * span * width * 2, transcendentals=0),
    )(*[pltpu.with_memory_space_constraint(x, pltpu.VMEM) for x in results])
    return (grad_input.reshape(level_input.shape), grad_filters, grad_mixing.transpose(1, 0, 2))


def solution(mesh):
    return jax.shard_map(
        body,
        mesh=mesh,
        in_specs=(
            P("dp", "ctx", None),
            P(None, "dp", "ctx", None),
            P(None, "dp", "ctx", None),
            P(),
            P(),
            P("dp", "ctx", None),
        ),
        out_specs=(P("dp", "ctx", None), P(), P()),
        check_vma=False,
    )
```

```python
import functools
import math

import jax
import jax.numpy as jnp
from jax import lax
from jax.experimental import pallas as pl
from jax.experimental.pallas import tpu as pltpu
from jax.sharding import PartitionSpec as P

BASE = 128
STRIP = 16
TILE = 8
LANES = 128
GROUP = 4
HALVES = 2
AHEAD = 3
MESH = pl.DeviceIdType.MESH
F32 = jnp.float32


def kernel(
    dims,
    cot,
    first,
    fwd,
    rev,
    filt_in,
    mix_in,
    out,
    out_filt,
    out_mix,
    dy,
    inputs,
    filt,
    mix,
    dy_wide,
    inputs_wide,
    partial,
    plain_sums,
    sums,
    coef,
    buf_a,
    buf_b,
    load_sem,
    send_sem,
    recv_sem,
    send_a,
    recv_a,
    send_b,
    recv_b,
):
    n_dp, n_ctx, units, levels, rows, factor = dims
    chunks = BASE // rows
    groups = n_ctx // GROUP
    width = dy.shape[-1]
    top = levels - 1

    dp = lax.axis_index("dp")
    me = lax.axis_index("ctx")
    q = lax.div(me, GROUP)
    r = lax.rem(me, GROUP)
    half = lax.div(r, 2)
    core = lax.rem(r, 2)
    outer = half == core
    sibling = me + 1 - 2 * core
    partner = me + 2 - 4 * half
    has_next = q < groups - 1
    has_prev = q > 0
    lower = half == 0
    z_sends = jnp.logical_or(jnp.logical_and(lower, has_next), jnp.logical_and(half == 1, has_prev))
    z_recvs = jnp.logical_or(jnp.logical_and(lower, has_prev), jnp.logical_and(half == 1, has_next))

    own_load = pltpu.make_async_copy(cot, dy.at[2], load_sem.at[0])
    in_loads = [
        pltpu.make_async_copy(first, inputs.at[0], load_sem.at[1]),
        pltpu.make_async_copy(fwd, inputs.at[pl.ds(1, top)], load_sem.at[2]),
        pltpu.make_async_copy(rev, inputs.at[pl.ds(levels, top)], load_sem.at[3]),
    ]
    small_loads = [
        pltpu.make_async_copy(filt_in, filt, load_sem.at[4]),
        pltpu.make_async_copy(mix_in, mix, load_sem.at[5]),
    ]
    for load in small_loads + [own_load] + in_loads:
        load.start()

    barrier = pltpu.get_barrier_semaphore()
    team = [(a, b) for a in range(n_dp) for b in range(GROUP) if (a, b) != (0, 0)]

    def team_member(a, b):
        return lax.rem(dp + a, n_dp), lax.rem(r + b, GROUP)

    for a, b in team:
        to_dp, to_r = team_member(a, b)
        pl.semaphore_signal(barrier, inc=1, device_id=(to_dp, q * GROUP + to_r), device_id_type=MESH)
    for k in range(1, groups):
        to_q = lax.rem(q + k, groups)
        pl.semaphore_signal(barrier, inc=1, device_id=(dp, to_q * GROUP + r), device_id_type=MESH)
    pl.semaphore_wait(barrier, len(team) + groups - 1)

    def part(ref, c, h):
        some = units // HALVES
        return ref.at[pl.ds(h * some, some), pl.ds(pl.multiple_of(c * rows, rows), rows), :]

    def hop(kind, c, h):
        if kind == 0:
            src, slot, to = cot, 4 * half, partner
        elif kind == 1:
            src, slot, to = cot, 1 + 2 * core, sibling
        elif kind == 2:
            src, slot, to = dy.at[4 - 4 * half], 4 * half, me + 4 - 8 * half
        else:
            src, slot, to = dy.at[4 - 4 * core], 3 - 2 * core, sibling
        return pltpu.make_async_remote_copy(
            src_ref=part(src, c, h),
            dst_ref=part(dy.at[slot], c, h),
            send_sem=send_sem.at[kind, c, h],
            recv_sem=recv_sem.at[kind, c, h],
            device_id=(dp, to),
            device_id_type=MESH,
        )

    def send_own(c):
        for kind in range(2):
            for h in range(HALVES):
                hop(kind, c, h).start()

    ahead = min(AHEAD, chunks)
    for c in range(ahead):
        send_own(c)

    @pl.when(jnp.logical_not(z_recvs))
    def _():
        dy[4 * half] = jnp.zeros(dy.shape[1:], dy.dtype)

    @pl.when(jnp.logical_and(jnp.logical_not(z_recvs), outer))
    def _():
        dy[1 + 2 * core] = jnp.zeros(dy.shape[1:], dy.dtype)

    for load in small_loads:
        load.wait()

    def weight(b, level):
        return mix[level, b : b + 1, :]

    for b in range(2):
        f00, f01 = filt[b, 0, 0:1, :], filt[b, 0, 1:2, :]
        f10, f11 = filt[b, 1, 0:1, :], filt[b, 1, 1:2, :]
        last, w = weight(b, levels), weight(b, top)
        values = [f01, f00, f01 * last + f11 * w, f00 * last + f10 * w]
        for level in range(top):
            w = weight(b, level)
            values += [f11 * w, f10 * w]
        for k, value in enumerate(values):
            coef[b, k] = jnp.broadcast_to(value, coef.shape[2:])
    sums[...] = jnp.zeros(sums.shape, F32)
    plain_sums[...] = jnp.zeros(plain_sums.shape, F32)

    lane_blocks = width // LANES

    def pieces(first_row, n_rows, size, work):
        @pl.loop(0, (n_rows // size) * lane_blocks)
        def _(piece):
            row = pl.multiple_of(lax.div(piece, lane_blocks) * size, size)
            lane = pl.multiple_of(lax.rem(piece, lane_blocks) * LANES, LANES)
            at = pl.ds(pl.multiple_of(first_row + row, size), size)
            work(at, pl.ds(row, size), pl.ds(lane, LANES))

    def place(b, m):
        return b * (units - 1) + (1 - 2 * b) * (m % units)

    def prepare(rows_at, _, lanes_at):
        own = []
        for j in range(units):
            own.append(dy[2, j, rows_at, lanes_at].astype(F32))
            for b in range(2):
                dy_wide[b, place(b, j), rows_at, lanes_at] = own[j]
        for slot in range(2 * levels - 1):
            level = slot if slot < levels else slot - top
            t_y = None
            for j in range(units):
                p = inputs[slot, j, rows_at, lanes_at].astype(F32)
                if slot < levels:
                    inputs_wide[0, level, j, rows_at, lanes_at] = p
                if slot == 0 or slot >= levels:
                    inputs_wide[1, level, place(1, j), rows_at, lanes_at] = p
                t_y = own[j] * p if t_y is None else t_y + own[j] * p
            plain_sums[slot, :, lanes_at] += t_y[:TILE] + t_y[TILE:]

    def widen(b, rows_at, _, lanes_at):
        for m in range(units, units + 2**levels - 1):
            strip = dy[2 + (1 - 2 * b) * (m // units), place(b, m), rows_at, lanes_at]
            dy_wide[b, m, rows_at, lanes_at] = strip.astype(F32)

    def branch(b, last, rows_at, _, lanes_at):
        def dy_at(m):
            return dy_wide[b, m, rows_at, lanes_at]

        def input_at(level, m):
            return inputs_wide[b, level, m, rows_at, lanes_at]

        def factor_at(k):
            return coef[b, k, :, lanes_at]

        def add(k, value):
            sums[b, k, :, lanes_at] += value

        shift = 2**top
        y = [dy_at(m) for m in range(units + 2 * shift - 1)]
        s_y = None
        for m in range(units):
            s = y[m + shift] * input_at(top, m)
            s_y = s if s_y is None else s_y + s
        add(0, s_y)
        here, there = factor_at(2), factor_at(3)
        g = [here * y[m] + there * y[m + shift] for m in range(units + shift - 1)]
        for level in reversed(range(top)):
            shift = 2**level
            y = [dy_at(m) for m in range(units + 2 * shift - 1)]
            acc = None
            for m in range(units):
                p = input_at(level, m)
                terms = [g[m + shift] * p, y[m + shift] * p, g[m] * p]
                acc = terms if acc is None else [u + v for u, v in zip(acc, terms)]
            for k in range(3):
                add(1 + 3 * level + k, acc[k])
            f01, f00 = factor_at(0), factor_at(1)
            w1, w0 = factor_at(4 + 2 * level), factor_at(5 + 2 * level)
            g = [
                f01 * g[m] + w1 * y[m] + (f00 * g[m + shift] + w0 * y[m + shift])
                for m in range(units + shift - 1)
            ]
        for m in range(units):
            if last:
                partial[units - 1 - m, rows_at, lanes_at] += g[m]
            else:
                partial[m, rows_at, lanes_at] = g[m]

    def finish(rows_at, _, lanes_at):
        for j in range(units):
            out[place(half, j), rows_at, lanes_at] = partial[j, rows_at, lanes_at].astype(out.dtype)

    own_load.wait()
    for load in in_loads:
        load.wait()
    pieces(0, BASE, STRIP, prepare)

    soon, mid, late = 1, 2, 3

    @pl.loop(0, chunks + late)
    def _(step):
        @pl.when(step < chunks)
        def _():
            for h in range(HALVES):
                hop(0, step, h).wait_recv()

                @pl.when(z_sends)
                def _():
                    hop(2, step, h).start()

                @pl.when(outer)
                def _():
                    hop(3, step, h).start()

            @pl.when(step + ahead < chunks)
            def _():
                send_own(step + ahead)

        @pl.when(jnp.logical_and(step >= mid, step < chunks + mid))
        def _():
            c = step - mid

            @pl.when(z_recvs)
            def _():
                for h in range(HALVES):
                    hop(2, c, h).wait_recv()

                    @pl.when(jnp.logical_not(outer))
                    def _():
                        hop(3, c, h).start()

        @pl.when(jnp.logical_and(step >= soon, step < chunks + soon))
        def _():
            c = step - soon
            for h in range(HALVES):
                hop(1, c, h).wait_recv()

            @pl.when(jnp.logical_not(outer))
            def _():
                for h in range(HALVES):
                    hop(3, c, h).wait_recv()

            pieces(c * rows, rows, STRIP, functools.partial(widen, half))
            pieces(c * rows, rows, TILE, functools.partial(branch, half, False))

        @pl.when(step >= late)
        def _():
            c = step - late

            @pl.when(jnp.logical_and(outer, z_recvs))
            def _():
                for h in range(HALVES):
                    hop(3, c, h).wait_recv()

            pieces(c * rows, rows, STRIP, functools.partial(widen, 1 - half))
            pieces(c * rows, rows, TILE, functools.partial(branch, 1 - half, True))
            pieces(c * rows, rows, STRIP, finish)

    slot_a = dp * GROUP + r
    n_filt = 8
    for b in range(2):
        f00, f01 = filt[b, 0, 0:1, :], filt[b, 0, 1:2, :]
        f10, f11 = filt[b, 1, 0:1, :], filt[b, 1, 1:2, :]

        def total(k):
            return jnp.sum(sums[b, k], axis=0, keepdims=True)

        def plain_total(level):
            slot = 0 if level == 0 else level + top * b
            return jnp.sum(plain_sums[slot], axis=0, keepdims=True)

        def put(k, value):
            buf_a[slot_a, k : k + 1, :] = value

        s_y, t_y = total(0), plain_total(top)
        last, w = weight(b, levels), weight(b, top)
        terms = [last * s_y, last * t_y, w * s_y, w * t_y]
        base = n_filt + b * (levels + 1)
        put(base + levels, f00 * s_y + f01 * t_y)
        put(base + top, f10 * s_y + f11 * t_y)
        for level in reversed(range(top)):
            s_a, s_y, t_a = [total(1 + 3 * level + k) for k in range(3)]
            t_y = plain_total(level)
            w = weight(b, level)
            terms = [u + v for u, v in zip(terms, [s_a, t_a, w * s_y, w * t_y])]
            put(base + level, f10 * s_y + f11 * t_y)
        for k in range(4):
            put(4 * b + k, terms[k])

    def team_copy(a, b):
        to_dp, to_r = team_member(a, b)
        slot = dp * GROUP + r
        return pltpu.make_async_remote_copy(
            src_ref=buf_a.at[slot],
            dst_ref=buf_a.at[slot],
            send_sem=send_a.at[a * GROUP + b],
            recv_sem=recv_a.at[a * GROUP + b],
            device_id=(to_dp, q * GROUP + to_r),
            device_id_type=MESH,
        )

    def group_copy(k):
        to_q = lax.rem(q + k, groups)
        return pltpu.make_async_remote_copy(
            src_ref=buf_b.at[q],
            dst_ref=buf_b.at[q],
            send_sem=send_b.at[k],
            recv_sem=recv_b.at[k],
            device_id=(dp, to_q * GROUP + r),
            device_id_type=MESH,
        )

    for a, b in team:
        team_copy(a, b).start()

    @pl.loop(0, chunks)
    def _(c):
        for h in range(HALVES):
            hop(0, c, h).wait_send()
            hop(1, c, h).wait_send()

            @pl.when(z_sends)
            def _():
                hop(2, c, h).wait_send()

            @pl.when(jnp.logical_or(outer, z_recvs))
            def _():
                hop(3, c, h).wait_send()

    for a, b in team:
        team_copy(a, b).wait_recv()
    value = buf_a[0]
    for k in range(1, n_dp * GROUP):
        value = value + buf_a[k]
    buf_b[q] = value
    for k in range(1, groups):
        group_copy(k).start()
    for k in range(1, groups):
        group_copy(k).wait_recv()
    value = buf_b[0]
    for k in range(1, groups):
        value = value + buf_b[k]
    value = value * factor
    for b in range(2):
        for kind in range(2):
            at = 4 * b + 2 * kind
            out_filt[b, kind] = value[at : at + 2]
        base = n_filt + b * (levels + 1)
        out_mix[:, b] = value[base : base + levels + 1]

    for a, b in team:
        team_copy(a, b).wait_send()
    for k in range(1, groups):
        group_copy(k).wait_send()


def hand_over(*refs):
    sources, targets, sem = refs[:3], refs[3:6], refs[6]
    copies = [pltpu.make_async_copy(sources[k], targets[k], sem.at[k]) for k in range(3)]
    for copy in copies:
        copy.start()
    for copy in copies:
        copy.wait()


def body(level_input, saved_forward, saved_reverse, filters, mixing, cotangent):
    n_dp, n_ctx = lax.axis_size("dp"), lax.axis_size("ctx")
    levels = saved_forward.shape[0] + 1
    seqs, span, width = level_input.shape
    units = span // BASE
    assert seqs == 1 and span % BASE == 0 and n_ctx % GROUP == 0
    assert units % HALVES == 0
    assert 2**levels <= 2 * units and width % LANES == 0
    rows = STRIP
    chunks = BASE // rows
    top = levels - 1
    groups = n_ctx // GROUP
    factor = 1.0 / math.sqrt(seqs * n_dp * span * n_ctx)
    terms = 8 + 2 * (levels + 1)
    block = (units, BASE, width)
    by_level = mixing.transpose(1, 0, 2)
    dma = pltpu.SemaphoreType.DMA
    hbm = pl.BlockSpec(memory_space=pltpu.HBM)
    vmem = pl.BlockSpec(memory_space=pltpu.VMEM)
    grad_input, grad_filters, grad_mixing = pl.pallas_call(
        functools.partial(kernel, (n_dp, n_ctx, units, levels, rows, factor)),
        out_shape=(
            pltpu.VMEM(block, jnp.bfloat16),
            pltpu.VMEM(filters.shape, F32),
            pltpu.VMEM(by_level.shape, F32),
        ),
        in_specs=[hbm] * 6,
        out_specs=(vmem, vmem, vmem),
        scratch_shapes=[
            pltpu.VMEM((5,) + block, jnp.bfloat16),
            pltpu.VMEM((2 * levels - 1,) + block, jnp.bfloat16),
            pltpu.VMEM(filters.shape, F32),
            pltpu.VMEM(by_level.shape, F32),
            pltpu.VMEM((2, units + 2**levels - 1, BASE, width), F32),
            pltpu.VMEM((2, levels) + block, F32),
            pltpu.VMEM(block, F32),
            pltpu.VMEM((2 * levels - 1, TILE, width), F32),
            pltpu.VMEM((2, 1 + 3 * top, TILE, width), F32),
            pltpu.VMEM((2, 4 + 2 * top, TILE, width), F32),
            pltpu.VMEM((n_dp * GROUP, terms, width), F32),
            pltpu.VMEM((groups, terms, width), F32),
            dma((6,)),
            dma((4, chunks, HALVES)),
            dma((4, chunks, HALVES)),
            dma((n_dp * GROUP,)),
            dma((n_dp * GROUP,)),
            dma((groups,)),
            dma((groups,)),
        ],
        compiler_params=pltpu.CompilerParams(
            collective_id=0, has_side_effects=True, vmem_limit_bytes=32 * 1024 * 1024
        ),
        cost_estimate=pl.CostEstimate(
            flops=300 * span * width, bytes_accessed=9 * span * width * 2, transcendentals=0
        ),
    )(
        *[
            pltpu.with_memory_space_constraint(operand, pltpu.HBM)
            for operand in (
                cotangent.reshape(block),
                level_input.reshape(block),
                saved_forward.reshape((top,) + block),
                saved_reverse.reshape((top,) + block),
                filters,
                by_level,
            )
        ]
    )
    results = (grad_input, grad_filters, grad_mixing)
    grad_input, grad_filters, grad_mixing = pl.pallas_call(
        hand_over,
        out_shape=tuple(pltpu.HBM(x.shape, x.dtype) for x in results),
        in_specs=[vmem] * 3,
        out_specs=(hbm,) * 3,
        scratch_shapes=[dma((3,))],
        cost_estimate=pl.CostEstimate(flops=0, bytes_accessed=2 * span * width * 2, transcendentals=0),
    )(*[pltpu.with_memory_space_constraint(x, pltpu.VMEM) for x in results])
    return (grad_input.reshape(level_input.shape), grad_filters, grad_mixing.transpose(1, 0, 2))


def solution(mesh):
    return jax.shard_map(
        body,
        mesh=mesh,
        in_specs=(
            P("dp", "ctx", None),
            P(None, "dp", "ctx", None),
            P(None, "dp", "ctx", None),
            P(),
            P(),
            P("dp", "ctx", None),
        ),
        out_specs=(P("dp", "ctx", None), P(), P()),
        check_vma=False,
    )
```

```python
import functools
import math

import jax
import jax.numpy as jnp
from jax import lax
from jax.experimental import pallas as pl
from jax.experimental.pallas import tpu as pltpu
from jax.sharding import PartitionSpec as P

BASE = 128
STRIP = 16
TILE = 8
LANES = 128
GROUP = 4
HALVES = 2
AHEAD = 2
MESH = pl.DeviceIdType.MESH
F32 = jnp.float32


def kernel(
    dims,
    cot,
    first,
    fwd,
    rev,
    filt_in,
    mix_in,
    out,
    out_filt,
    out_mix,
    dy,
    inputs,
    filt,
    mix,
    dy_wide,
    inputs_wide,
    partial,
    plain_sums,
    sums,
    coef,
    buf_a,
    buf_b,
    load_sem,
    send_sem,
    recv_sem,
    send_a,
    recv_a,
    send_b,
    recv_b,
):
    n_dp, n_ctx, units, levels, rows, factor = dims
    chunks = BASE // rows
    groups = n_ctx // GROUP
    width = dy.shape[-1]
    top = levels - 1

    dp = lax.axis_index("dp")
    me = lax.axis_index("ctx")
    q = lax.div(me, GROUP)
    r = lax.rem(me, GROUP)
    half = lax.div(r, 2)
    core = lax.rem(r, 2)
    outer = half == core
    sibling = me + 1 - 2 * core
    partner = me + 2 - 4 * half
    has_next = q < groups - 1
    has_prev = q > 0
    lower = half == 0
    z_sends = jnp.logical_or(jnp.logical_and(lower, has_next), jnp.logical_and(half == 1, has_prev))
    z_recvs = jnp.logical_or(jnp.logical_and(lower, has_prev), jnp.logical_and(half == 1, has_next))

    own_load = pltpu.make_async_copy(cot, dy.at[2], load_sem.at[0])
    in_loads = [
        pltpu.make_async_copy(first, inputs.at[0], load_sem.at[1]),
        pltpu.make_async_copy(fwd, inputs.at[pl.ds(1, top)], load_sem.at[2]),
        pltpu.make_async_copy(rev, inputs.at[pl.ds(levels, top)], load_sem.at[3]),
    ]
    small_loads = [
        pltpu.make_async_copy(filt_in, filt, load_sem.at[4]),
        pltpu.make_async_copy(mix_in, mix, load_sem.at[5]),
    ]
    for load in small_loads + [own_load] + in_loads:
        load.start()

    barrier = pltpu.get_barrier_semaphore()
    team = [(a, b) for a in range(n_dp) for b in range(GROUP) if (a, b) != (0, 0)]

    def team_member(a, b):
        return lax.rem(dp + a, n_dp), lax.rem(r + b, GROUP)

    for a, b in team:
        to_dp, to_r = team_member(a, b)
        pl.semaphore_signal(barrier, inc=1, device_id=(to_dp, q * GROUP + to_r), device_id_type=MESH)
    for k in range(1, groups):
        to_q = lax.rem(q + k, groups)
        pl.semaphore_signal(barrier, inc=1, device_id=(dp, to_q * GROUP + r), device_id_type=MESH)
    pl.semaphore_wait(barrier, len(team) + groups - 1)

    def part(ref, c, h):
        some = units // HALVES
        return ref.at[pl.ds(h * some, some), pl.ds(pl.multiple_of(c * rows, rows), rows), :]

    def hop(kind, c, h):
        if kind == 0:
            src, slot, to = cot, 4 * half, partner
        elif kind == 1:
            src, slot, to = cot, 1 + 2 * core, sibling
        elif kind == 2:
            src, slot, to = dy.at[4 - 4 * half], 4 * half, me + 4 - 8 * half
        else:
            src, slot, to = dy.at[4 - 4 * core], 3 - 2 * core, sibling
        return pltpu.make_async_remote_copy(
            src_ref=part(src, c, h),
            dst_ref=part(dy.at[slot], c, h),
            send_sem=send_sem.at[kind, c, h],
            recv_sem=recv_sem.at[kind, c, h],
            device_id=(dp, to),
            device_id_type=MESH,
        )

    def send_own(c):
        for kind in range(2):
            for h in range(HALVES):
                hop(kind, c, h).start()

    ahead = min(AHEAD, chunks)
    for c in range(ahead):
        send_own(c)

    @pl.when(jnp.logical_not(z_recvs))
    def _():
        dy[4 * half] = jnp.zeros(dy.shape[1:], dy.dtype)

    @pl.when(jnp.logical_and(jnp.logical_not(z_recvs), outer))
    def _():
        dy[1 + 2 * core] = jnp.zeros(dy.shape[1:], dy.dtype)

    for load in small_loads:
        load.wait()

    def weight(b, level):
        return mix[level, b : b + 1, :]

    for b in range(2):
        f00, f01 = filt[b, 0, 0:1, :], filt[b, 0, 1:2, :]
        f10, f11 = filt[b, 1, 0:1, :], filt[b, 1, 1:2, :]
        last, w = weight(b, levels), weight(b, top)
        values = [f01, f00, f01 * last + f11 * w, f00 * last + f10 * w]
        for level in range(top):
            w = weight(b, level)
            values += [f11 * w, f10 * w]
        for k, value in enumerate(values):
            coef[b, k] = jnp.broadcast_to(value, coef.shape[2:])
    sums[...] = jnp.zeros(sums.shape, F32)
    plain_sums[...] = jnp.zeros(plain_sums.shape, F32)

    lane_blocks = width // LANES

    def pieces(first_row, n_rows, size, work):
        @pl.loop(0, (n_rows // size) * lane_blocks)
        def _(piece):
            row = pl.multiple_of(lax.div(piece, lane_blocks) * size, size)
            lane = pl.multiple_of(lax.rem(piece, lane_blocks) * LANES, LANES)
            at = pl.ds(pl.multiple_of(first_row + row, size), size)
            work(at, pl.ds(row, size), pl.ds(lane, LANES))

    def place(b, m):
        return b * (units - 1) + (1 - 2 * b) * (m % units)

    def prepare(rows_at, _, lanes_at):
        own = []
        for j in range(units):
            own.append(dy[2, j, rows_at, lanes_at].astype(F32))
            for b in range(2):
                dy_wide[b, place(b, j), rows_at, lanes_at] = own[j]
        for slot in range(2 * levels - 1):
            level = slot if slot < levels else slot - top
            t_y = None
            for j in range(units):
                p = inputs[slot, j, rows_at, lanes_at].astype(F32)
                if slot < levels:
                    inputs_wide[0, level, j, rows_at, lanes_at] = p
                if slot == 0 or slot >= levels:
                    inputs_wide[1, level, place(1, j), rows_at, lanes_at] = p
                t_y = own[j] * p if t_y is None else t_y + own[j] * p
            plain_sums[slot, :, lanes_at] += t_y[:TILE] + t_y[TILE:]

    def widen(b, rows_at, _, lanes_at):
        for m in range(units, units + 2**levels - 1):
            strip = dy[2 + (1 - 2 * b) * (m // units), place(b, m), rows_at, lanes_at]
            dy_wide[b, m, rows_at, lanes_at] = strip.astype(F32)

    def branch(b, last, rows_at, _, lanes_at):
        def dy_at(m):
            return dy_wide[b, m, rows_at, lanes_at]

        def input_at(level, m):
            return inputs_wide[b, level, m, rows_at, lanes_at]

        def factor_at(k):
            return coef[b, k, 0:1, lanes_at]

        def add(k, value):
            sums[b, k, :, lanes_at] += value[:TILE] + value[TILE:]

        shift = 2**top
        y = [dy_at(m) for m in range(units + 2 * shift - 1)]
        s_y = None
        for m in range(units):
            s = y[m + shift] * input_at(top, m)
            s_y = s if s_y is None else s_y + s
        add(0, s_y)
        here, there = factor_at(2), factor_at(3)
        g = [here * y[m] + there * y[m + shift] for m in range(units + shift - 1)]
        for level in reversed(range(top)):
            shift = 2**level
            y = [dy_at(m) for m in range(units + 2 * shift - 1)]
            acc = None
            for m in range(units):
                p = input_at(level, m)
                terms = [g[m + shift] * p, y[m + shift] * p, g[m] * p]
                acc = terms if acc is None else [u + v for u, v in zip(acc, terms)]
            for k in range(3):
                add(1 + 3 * level + k, acc[k])
            f01, f00 = factor_at(0), factor_at(1)
            w1, w0 = factor_at(4 + 2 * level), factor_at(5 + 2 * level)
            g = [
                f01 * g[m] + w1 * y[m] + (f00 * g[m + shift] + w0 * y[m + shift])
                for m in range(units + shift - 1)
            ]
        for m in range(units):
            if last:
                partial[units - 1 - m, rows_at, lanes_at] += g[m]
            else:
                partial[m, rows_at, lanes_at] = g[m]

    def finish(rows_at, _, lanes_at):
        for j in range(units):
            out[place(half, j), rows_at, lanes_at] = partial[j, rows_at, lanes_at].astype(out.dtype)

    own_load.wait()
    for load in in_loads:
        load.wait()
    pieces(0, BASE, STRIP, prepare)

    soon, mid, late = 1, 1, 2

    @pl.loop(0, chunks + late)
    def _(step):
        @pl.when(step < chunks)
        def _():
            for h in range(HALVES):
                hop(0, step, h).wait_recv()

                @pl.when(z_sends)
                def _():
                    hop(2, step, h).start()

                @pl.when(outer)
                def _():
                    hop(3, step, h).start()

            @pl.when(step + ahead < chunks)
            def _():
                send_own(step + ahead)

        @pl.when(jnp.logical_and(step >= mid, step < chunks + mid))
        def _():
            c = step - mid

            @pl.when(z_recvs)
            def _():
                for h in range(HALVES):
                    hop(2, c, h).wait_recv()

                    @pl.when(jnp.logical_not(outer))
                    def _():
                        hop(3, c, h).start()

        @pl.when(jnp.logical_and(step >= soon, step < chunks + soon))
        def _():
            c = step - soon
            for h in range(HALVES):
                hop(1, c, h).wait_recv()

            @pl.when(jnp.logical_not(outer))
            def _():
                for h in range(HALVES):
                    hop(3, c, h).wait_recv()

            pieces(c * rows, rows, STRIP, functools.partial(widen, half))
            pieces(c * rows, rows, STRIP, functools.partial(branch, half, False))

        @pl.when(step >= late)
        def _():
            c = step - late

            @pl.when(jnp.logical_and(outer, z_recvs))
            def _():
                for h in range(HALVES):
                    hop(3, c, h).wait_recv()

            pieces(c * rows, rows, STRIP, functools.partial(widen, 1 - half))
            pieces(c * rows, rows, STRIP, functools.partial(branch, 1 - half, True))
            pieces(c * rows, rows, STRIP, finish)

    slot_a = dp * GROUP + r
    n_filt = 8
    for b in range(2):
        f00, f01 = filt[b, 0, 0:1, :], filt[b, 0, 1:2, :]
        f10, f11 = filt[b, 1, 0:1, :], filt[b, 1, 1:2, :]

        def total(k):
            return jnp.sum(sums[b, k], axis=0, keepdims=True)

        def plain_total(level):
            slot = 0 if level == 0 else level + top * b
            return jnp.sum(plain_sums[slot], axis=0, keepdims=True)

        def put(k, value):
            buf_a[slot_a, k : k + 1, :] = value

        s_y, t_y = total(0), plain_total(top)
        last, w = weight(b, levels), weight(b, top)
        terms = [last * s_y, last * t_y, w * s_y, w * t_y]
        base = n_filt + b * (levels + 1)
        put(base + levels, f00 * s_y + f01 * t_y)
        put(base + top, f10 * s_y + f11 * t_y)
        for level in reversed(range(top)):
            s_a, s_y, t_a = [total(1 + 3 * level + k) for k in range(3)]
            t_y = plain_total(level)
            w = weight(b, level)
            terms = [u + v for u, v in zip(terms, [s_a, t_a, w * s_y, w * t_y])]
            put(base + level, f10 * s_y + f11 * t_y)
        for k in range(4):
            put(4 * b + k, terms[k])

    def team_copy(a, b):
        to_dp, to_r = team_member(a, b)
        slot = dp * GROUP + r
        return pltpu.make_async_remote_copy(
            src_ref=buf_a.at[slot],
            dst_ref=buf_a.at[slot],
            send_sem=send_a.at[a * GROUP + b],
            recv_sem=recv_a.at[a * GROUP + b],
            device_id=(to_dp, q * GROUP + to_r),
            device_id_type=MESH,
        )

    def group_copy(k):
        to_q = lax.rem(q + k, groups)
        return pltpu.make_async_remote_copy(
            src_ref=buf_b.at[q],
            dst_ref=buf_b.at[q],
            send_sem=send_b.at[k],
            recv_sem=recv_b.at[k],
            device_id=(dp, to_q * GROUP + r),
            device_id_type=MESH,
        )

    for a, b in team:
        team_copy(a, b).start()

    @pl.loop(0, chunks)
    def _(c):
        for h in range(HALVES):
            hop(0, c, h).wait_send()
            hop(1, c, h).wait_send()

            @pl.when(z_sends)
            def _():
                hop(2, c, h).wait_send()

            @pl.when(jnp.logical_or(outer, z_recvs))
            def _():
                hop(3, c, h).wait_send()

    for a, b in team:
        team_copy(a, b).wait_recv()
    value = buf_a[0]
    for k in range(1, n_dp * GROUP):
        value = value + buf_a[k]
    buf_b[q] = value
    for k in range(1, groups):
        group_copy(k).start()
    for k in range(1, groups):
        group_copy(k).wait_recv()
    value = buf_b[0]
    for k in range(1, groups):
        value = value + buf_b[k]
    value = value * factor
    for b in range(2):
        for kind in range(2):
            at = 4 * b + 2 * kind
            out_filt[b, kind] = value[at : at + 2]
        base = n_filt + b * (levels + 1)
        out_mix[:, b] = value[base : base + levels + 1]

    for a, b in team:
        team_copy(a, b).wait_send()
    for k in range(1, groups):
        group_copy(k).wait_send()


def hand_over(*refs):
    sources, targets, sem = refs[:3], refs[3:6], refs[6]
    copies = [pltpu.make_async_copy(sources[k], targets[k], sem.at[k]) for k in range(3)]
    for copy in copies:
        copy.start()
    for copy in copies:
        copy.wait()


def body(level_input, saved_forward, saved_reverse, filters, mixing, cotangent):
    n_dp, n_ctx = lax.axis_size("dp"), lax.axis_size("ctx")
    levels = saved_forward.shape[0] + 1
    seqs, span, width = level_input.shape
    units = span // BASE
    assert seqs == 1 and span % BASE == 0 and n_ctx % GROUP == 0
    assert units % HALVES == 0
    assert 2**levels <= 2 * units and width % LANES == 0
    rows = 2 * STRIP
    chunks = BASE // rows
    top = levels - 1
    groups = n_ctx // GROUP
    factor = 1.0 / math.sqrt(seqs * n_dp * span * n_ctx)
    terms = 8 + 2 * (levels + 1)
    block = (units, BASE, width)
    by_level = mixing.transpose(1, 0, 2)
    dma = pltpu.SemaphoreType.DMA
    hbm = pl.BlockSpec(memory_space=pltpu.HBM)
    vmem = pl.BlockSpec(memory_space=pltpu.VMEM)
    grad_input, grad_filters, grad_mixing = pl.pallas_call(
        functools.partial(kernel, (n_dp, n_ctx, units, levels, rows, factor)),
        out_shape=(
            pltpu.VMEM(block, jnp.bfloat16),
            pltpu.VMEM(filters.shape, F32),
            pltpu.VMEM(by_level.shape, F32),
        ),
        in_specs=[hbm] * 6,
        out_specs=(vmem, vmem, vmem),
        scratch_shapes=[
            pltpu.VMEM((5,) + block, jnp.bfloat16),
            pltpu.VMEM((2 * levels - 1,) + block, jnp.bfloat16),
            pltpu.VMEM(filters.shape, F32),
            pltpu.VMEM(by_level.shape, F32),
            pltpu.VMEM((2, units + 2**levels - 1, BASE, width), F32),
            pltpu.VMEM((2, levels) + block, F32),
            pltpu.VMEM(block, F32),
            pltpu.VMEM((2 * levels - 1, TILE, width), F32),
            pltpu.VMEM((2, 1 + 3 * top, TILE, width), F32),
            pltpu.VMEM((2, 4 + 2 * top, TILE, width), F32),
            pltpu.VMEM((n_dp * GROUP, terms, width), F32),
            pltpu.VMEM((groups, terms, width), F32),
            dma((6,)),
            dma((4, chunks, HALVES)),
            dma((4, chunks, HALVES)),
            dma((n_dp * GROUP,)),
            dma((n_dp * GROUP,)),
            dma((groups,)),
            dma((groups,)),
        ],
        compiler_params=pltpu.CompilerParams(
            collective_id=0, has_side_effects=True, vmem_limit_bytes=32 * 1024 * 1024
        ),
        cost_estimate=pl.CostEstimate(
            flops=300 * span * width, bytes_accessed=9 * span * width * 2, transcendentals=0
        ),
    )(
        *[
            pltpu.with_memory_space_constraint(operand, pltpu.HBM)
            for operand in (
                cotangent.reshape(block),
                level_input.reshape(block),
                saved_forward.reshape((top,) + block),
                saved_reverse.reshape((top,) + block),
                filters,
                by_level,
            )
        ]
    )
    results = (grad_input, grad_filters, grad_mixing)
    grad_input, grad_filters, grad_mixing = pl.pallas_call(
        hand_over,
        out_shape=tuple(pltpu.HBM(x.shape, x.dtype) for x in results),
        in_specs=[vmem] * 3,
        out_specs=(hbm,) * 3,
        scratch_shapes=[dma((3,))],
        cost_estimate=pl.CostEstimate(flops=0, bytes_accessed=2 * span * width * 2, transcendentals=0),
    )(*[pltpu.with_memory_space_constraint(x, pltpu.VMEM) for x in results])
    return (grad_input.reshape(level_input.shape), grad_filters, grad_mixing.transpose(1, 0, 2))


def solution(mesh):
    return jax.shard_map(
        body,
        mesh=mesh,
        in_specs=(
            P("dp", "ctx", None),
            P(None, "dp", "ctx", None),
            P(None, "dp", "ctx", None),
            P(),
            P(),
            P("dp", "ctx", None),
        ),
        out_specs=(P("dp", "ctx", None), P(), P()),
        check_vma=False,
    )
```

```python
import functools
import math

import jax
import jax.numpy as jnp
from jax import lax
from jax.experimental import pallas as pl
from jax.experimental.pallas import tpu as pltpu
from jax.sharding import PartitionSpec as P

BASE = 128
STRIP = 16
TILE = 8
LANES = 128
GROUP = 4
HALVES = 2
AHEAD = 4
MESH = pl.DeviceIdType.MESH
F32 = jnp.float32


def kernel(
    dims,
    cot,
    first,
    fwd,
    rev,
    filt_in,
    mix_in,
    out,
    out_filt,
    out_mix,
    dy,
    inputs,
    filt,
    mix,
    dy_wide,
    inputs_wide,
    partial,
    plain_sums,
    sums,
    coef,
    buf_a,
    buf_b,
    load_sem,
    send_sem,
    recv_sem,
    send_a,
    recv_a,
    send_b,
    recv_b,
):
    n_dp, n_ctx, units, levels, rows, factor = dims
    chunks = BASE // rows
    groups = n_ctx // GROUP
    width = dy.shape[-1]
    top = levels - 1

    dp = lax.axis_index("dp")
    me = lax.axis_index("ctx")
    q = lax.div(me, GROUP)
    r = lax.rem(me, GROUP)
    half = lax.div(r, 2)
    core = lax.rem(r, 2)
    outer = half == core
    sibling = me + 1 - 2 * core
    partner = me + 2 - 4 * half
    has_next = q < groups - 1
    has_prev = q > 0
    lower = half == 0
    z_sends = jnp.logical_or(jnp.logical_and(lower, has_next), jnp.logical_and(half == 1, has_prev))
    z_recvs = jnp.logical_or(jnp.logical_and(lower, has_prev), jnp.logical_and(half == 1, has_next))

    own_load = pltpu.make_async_copy(cot, dy.at[2], load_sem.at[0])
    in_loads = [
        pltpu.make_async_copy(first, inputs.at[0], load_sem.at[1]),
        pltpu.make_async_copy(fwd, inputs.at[pl.ds(1, top)], load_sem.at[2]),
        pltpu.make_async_copy(rev, inputs.at[pl.ds(levels, top)], load_sem.at[3]),
    ]
    small_loads = [
        pltpu.make_async_copy(filt_in, filt, load_sem.at[4]),
        pltpu.make_async_copy(mix_in, mix, load_sem.at[5]),
    ]
    for load in small_loads + [own_load] + in_loads:
        load.start()

    barrier = pltpu.get_barrier_semaphore()
    team = [(a, b) for a in range(n_dp) for b in range(GROUP) if (a, b) != (0, 0)]

    def team_member(a, b):
        return lax.rem(dp + a, n_dp), lax.rem(r + b, GROUP)

    for a, b in team:
        to_dp, to_r = team_member(a, b)
        pl.semaphore_signal(barrier, inc=1, device_id=(to_dp, q * GROUP + to_r), device_id_type=MESH)
    for k in range(1, groups):
        to_q = lax.rem(q + k, groups)
        pl.semaphore_signal(barrier, inc=1, device_id=(dp, to_q * GROUP + r), device_id_type=MESH)
    pl.semaphore_wait(barrier, len(team) + groups - 1)

    def part(ref, c, h):
        some = units // HALVES
        return ref.at[pl.ds(h * some, some), pl.ds(pl.multiple_of(c * rows, rows), rows), :]

    def hop(kind, c, h):
        if kind == 0:
            src, slot, to = cot, 4 * half, partner
        elif kind == 1:
            src, slot, to = cot, 1 + 2 * core, sibling
        elif kind == 2:
            src, slot, to = dy.at[4 - 4 * half], 4 * half, me + 4 - 8 * half
        else:
            src, slot, to = dy.at[4 - 4 * core], 3 - 2 * core, sibling
        return pltpu.make_async_remote_copy(
            src_ref=part(src, c, h),
            dst_ref=part(dy.at[slot], c, h),
            send_sem=send_sem.at[kind, c, h],
            recv_sem=recv_sem.at[kind, c, h],
            device_id=(dp, to),
            device_id_type=MESH,
        )

    def send_own(c):
        for kind in range(2):
            for h in range(HALVES):
                hop(kind, c, h).start()

    ahead = min(AHEAD, chunks)
    for c in range(ahead):
        send_own(c)

    @pl.when(jnp.logical_not(z_recvs))
    def _():
        dy[4 * half] = jnp.zeros(dy.shape[1:], dy.dtype)

    @pl.when(jnp.logical_and(jnp.logical_not(z_recvs), outer))
    def _():
        dy[1 + 2 * core] = jnp.zeros(dy.shape[1:], dy.dtype)

    for load in small_loads:
        load.wait()

    def weight(b, level):
        return mix[level, b : b + 1, :]

    for b in range(2):
        f00, f01 = filt[b, 0, 0:1, :], filt[b, 0, 1:2, :]
        f10, f11 = filt[b, 1, 0:1, :], filt[b, 1, 1:2, :]
        last, w = weight(b, levels), weight(b, top)
        values = [f01, f00, f01 * last + f11 * w, f00 * last + f10 * w]
        for level in range(top):
            w = weight(b, level)
            values += [f11 * w, f10 * w]
        for k, value in enumerate(values):
            coef[b, k] = jnp.broadcast_to(value, coef.shape[2:])
    sums[...] = jnp.zeros(sums.shape, F32)
    plain_sums[...] = jnp.zeros(plain_sums.shape, F32)

    lane_blocks = width // LANES

    def pieces(first_row, n_rows, size, work):
        @pl.loop(0, (n_rows // size) * lane_blocks)
        def _(piece):
            row = pl.multiple_of(lax.div(piece, lane_blocks) * size, size)
            lane = pl.multiple_of(lax.rem(piece, lane_blocks) * LANES, LANES)
            at = pl.ds(pl.multiple_of(first_row + row, size), size)
            work(at, pl.ds(row, size), pl.ds(lane, LANES))

    def place(b, m):
        return b * (units - 1) + (1 - 2 * b) * (m % units)

    def prepare(rows_at, _, lanes_at):
        own = []
        for j in range(units):
            own.append(dy[2, j, rows_at, lanes_at].astype(F32))
            for b in range(2):
                dy_wide[b, place(b, j), rows_at, lanes_at] = own[j]
        for slot in range(2 * levels - 1):
            level = slot if slot < levels else slot - top
            t_y = None
            for j in range(units):
                p = inputs[slot, j, rows_at, lanes_at].astype(F32)
                if slot < levels:
                    inputs_wide[0, level, j, rows_at, lanes_at] = p
                if slot == 0 or slot >= levels:
                    inputs_wide[1, level, place(1, j), rows_at, lanes_at] = p
                t_y = own[j] * p if t_y is None else t_y + own[j] * p
            plain_sums[slot, :, lanes_at] += t_y[:TILE] + t_y[TILE:]

    def widen(b, rows_at, _, lanes_at):
        for m in range(units, units + 2**levels - 1):
            strip = dy[2 + (1 - 2 * b) * (m // units), place(b, m), rows_at, lanes_at]
            dy_wide[b, m, rows_at, lanes_at] = strip.astype(F32)

    def branch(b, last, rows_at, _, lanes_at):
        def dy_at(m):
            return dy_wide[b, m, rows_at, lanes_at]

        def input_at(level, m):
            return inputs_wide[b, level, m, rows_at, lanes_at]

        def factor_at(k):
            return coef[b, k, 0:1, lanes_at]

        def add(k, value):
            sums[b, k, :, lanes_at] += value[:TILE] + value[TILE:]

        shift = 2**top
        y = [dy_at(m) for m in range(units + 2 * shift - 1)]
        s_y = None
        for m in range(units):
            s = y[m + shift] * input_at(top, m)
            s_y = s if s_y is None else s_y + s
        add(0, s_y)
        here, there = factor_at(2), factor_at(3)
        g = [here * y[m] + there * y[m + shift] for m in range(units + shift - 1)]
        for level in reversed(range(top)):
            shift = 2**level
            y = [dy_at(m) for m in range(units + 2 * shift - 1)]
            acc = None
            for m in range(units):
                p = input_at(level, m)
                terms = [g[m + shift] * p, y[m + shift] * p, g[m] * p]
                acc = terms if acc is None else [u + v for u, v in zip(acc, terms)]
            for k in range(3):
                add(1 + 3 * level + k, acc[k])
            f01, f00 = factor_at(0), factor_at(1)
            w1, w0 = factor_at(4 + 2 * level), factor_at(5 + 2 * level)
            g = [
                f01 * g[m] + w1 * y[m] + (f00 * g[m + shift] + w0 * y[m + shift])
                for m in range(units + shift - 1)
            ]
        for m in range(units):
            if last:
                partial[units - 1 - m, rows_at, lanes_at] += g[m]
            else:
                partial[m, rows_at, lanes_at] = g[m]

    def finish(rows_at, _, lanes_at):
        for j in range(units):
            out[place(half, j), rows_at, lanes_at] = partial[j, rows_at, lanes_at].astype(out.dtype)

    own_load.wait()
    for load in in_loads:
        load.wait()
    early = chunks // 2
    pieces(0, early * rows, STRIP, prepare)

    soon, mid, late = 1, 2, 3

    @pl.loop(0, chunks + late)
    def _(step):
        def forward(h):
            @pl.when(step < chunks)
            def _():
                hop(0, step, h).wait_recv()

                @pl.when(z_sends)
                def _():
                    hop(2, step, h).start()

                @pl.when(outer)
                def _():
                    hop(3, step, h).start()

        forward(0)

        @pl.when(jnp.logical_and(step >= soon, step < chunks + soon))
        def _():
            c = step - soon
            for h in range(HALVES):
                hop(1, c, h).wait_recv()

            @pl.when(jnp.logical_not(outer))
            def _():
                for h in range(HALVES):
                    hop(3, c, h).wait_recv()

            pieces(c * rows, rows, STRIP, functools.partial(widen, half))
            pieces(c * rows, rows, STRIP, functools.partial(branch, half, False))

        for h in range(1, HALVES):
            forward(h)

        @pl.when(step + ahead < chunks)
        def _():
            send_own(step + ahead)

        @pl.when(step + early < chunks)
        def _():
            pieces((step + early) * rows, rows, STRIP, prepare)

        @pl.when(jnp.logical_and(step >= mid, step < chunks + mid))
        def _():
            c = step - mid

            @pl.when(z_recvs)
            def _():
                for h in range(HALVES):
                    hop(2, c, h).wait_recv()

                    @pl.when(jnp.logical_not(outer))
                    def _():
                        hop(3, c, h).start()

        @pl.when(step >= late)
        def _():
            c = step - late

            @pl.when(jnp.logical_and(outer, z_recvs))
            def _():
                for h in range(HALVES):
                    hop(3, c, h).wait_recv()

            pieces(c * rows, rows, STRIP, functools.partial(widen, 1 - half))
            pieces(c * rows, rows, STRIP, functools.partial(branch, 1 - half, True))
            pieces(c * rows, rows, STRIP, finish)

    slot_a = dp * GROUP + r
    n_filt = 8
    for b in range(2):
        f00, f01 = filt[b, 0, 0:1, :], filt[b, 0, 1:2, :]
        f10, f11 = filt[b, 1, 0:1, :], filt[b, 1, 1:2, :]

        def total(k):
            return jnp.sum(sums[b, k], axis=0, keepdims=True)

        def plain_total(level):
            slot = 0 if level == 0 else level + top * b
            return jnp.sum(plain_sums[slot], axis=0, keepdims=True)

        def put(k, value):
            buf_a[slot_a, k : k + 1, :] = value

        s_y, t_y = total(0), plain_total(top)
        last, w = weight(b, levels), weight(b, top)
        terms = [last * s_y, last * t_y, w * s_y, w * t_y]
        base = n_filt + b * (levels + 1)
        put(base + levels, f00 * s_y + f01 * t_y)
        put(base + top, f10 * s_y + f11 * t_y)
        for level in reversed(range(top)):
            s_a, s_y, t_a = [total(1 + 3 * level + k) for k in range(3)]
            t_y = plain_total(level)
            w = weight(b, level)
            terms = [u + v for u, v in zip(terms, [s_a, t_a, w * s_y, w * t_y])]
            put(base + level, f10 * s_y + f11 * t_y)
        for k in range(4):
            put(4 * b + k, terms[k])

    def team_copy(a, b):
        to_dp, to_r = team_member(a, b)
        slot = dp * GROUP + r
        return pltpu.make_async_remote_copy(
            src_ref=buf_a.at[slot],
            dst_ref=buf_a.at[slot],
            send_sem=send_a.at[a * GROUP + b],
            recv_sem=recv_a.at[a * GROUP + b],
            device_id=(to_dp, q * GROUP + to_r),
            device_id_type=MESH,
        )

    def group_copy(k):
        to_q = lax.rem(q + k, groups)
        return pltpu.make_async_remote_copy(
            src_ref=buf_b.at[q],
            dst_ref=buf_b.at[q],
            send_sem=send_b.at[k],
            recv_sem=recv_b.at[k],
            device_id=(dp, to_q * GROUP + r),
            device_id_type=MESH,
        )

    for a, b in team:
        team_copy(a, b).start()

    @pl.loop(0, chunks)
    def _(c):
        for h in range(HALVES):
            hop(0, c, h).wait_send()
            hop(1, c, h).wait_send()

            @pl.when(z_sends)
            def _():
                hop(2, c, h).wait_send()

            @pl.when(jnp.logical_or(outer, z_recvs))
            def _():
                hop(3, c, h).wait_send()

    for a, b in team:
        team_copy(a, b).wait_recv()
    value = buf_a[0]
    for k in range(1, n_dp * GROUP):
        value = value + buf_a[k]
    buf_b[q] = value
    for k in range(1, groups):
        group_copy(k).start()
    for k in range(1, groups):
        group_copy(k).wait_recv()
    value = buf_b[0]
    for k in range(1, groups):
        value = value + buf_b[k]
    value = value * factor
    for b in range(2):
        for kind in range(2):
            at = 4 * b + 2 * kind
            out_filt[b, kind] = value[at : at + 2]
        base = n_filt + b * (levels + 1)
        out_mix[:, b] = value[base : base + levels + 1]

    for a, b in team:
        team_copy(a, b).wait_send()
    for k in range(1, groups):
        group_copy(k).wait_send()


def hand_over(*refs):
    sources, targets, sem = refs[:3], refs[3:6], refs[6]
    copies = [pltpu.make_async_copy(sources[k], targets[k], sem.at[k]) for k in range(3)]
    for copy in copies:
        copy.start()
    for copy in copies:
        copy.wait()


def body(level_input, saved_forward, saved_reverse, filters, mixing, cotangent):
    n_dp, n_ctx = lax.axis_size("dp"), lax.axis_size("ctx")
    levels = saved_forward.shape[0] + 1
    seqs, span, width = level_input.shape
    units = span // BASE
    assert seqs == 1 and span % BASE == 0 and n_ctx % GROUP == 0
    assert units % HALVES == 0
    assert 2**levels <= 2 * units and width % LANES == 0
    rows = STRIP
    chunks = BASE // rows
    top = levels - 1
    groups = n_ctx // GROUP
    factor = 1.0 / math.sqrt(seqs * n_dp * span * n_ctx)
    terms = 8 + 2 * (levels + 1)
    block = (units, BASE, width)
    by_level = mixing.transpose(1, 0, 2)
    dma = pltpu.SemaphoreType.DMA
    hbm = pl.BlockSpec(memory_space=pltpu.HBM)
    vmem = pl.BlockSpec(memory_space=pltpu.VMEM)
    grad_input, grad_filters, grad_mixing = pl.pallas_call(
        functools.partial(kernel, (n_dp, n_ctx, units, levels, rows, factor)),
        out_shape=(
            pltpu.VMEM(block, jnp.bfloat16),
            pltpu.VMEM(filters.shape, F32),
            pltpu.VMEM(by_level.shape, F32),
        ),
        in_specs=[hbm] * 6,
        out_specs=(vmem, vmem, vmem),
        scratch_shapes=[
            pltpu.VMEM((5,) + block, jnp.bfloat16),
            pltpu.VMEM((2 * levels - 1,) + block, jnp.bfloat16),
            pltpu.VMEM(filters.shape, F32),
            pltpu.VMEM(by_level.shape, F32),
            pltpu.VMEM((2, units + 2**levels - 1, BASE, width), F32),
            pltpu.VMEM((2, levels) + block, F32),
            pltpu.VMEM(block, F32),
            pltpu.VMEM((2 * levels - 1, TILE, width), F32),
            pltpu.VMEM((2, 1 + 3 * top, TILE, width), F32),
            pltpu.VMEM((2, 4 + 2 * top, TILE, width), F32),
            pltpu.VMEM((n_dp * GROUP, terms, width), F32),
            pltpu.VMEM((groups, terms, width), F32),
            dma((6,)),
            dma((4, chunks, HALVES)),
            dma((4, chunks, HALVES)),
            dma((n_dp * GROUP,)),
            dma((n_dp * GROUP,)),
            dma((groups,)),
            dma((groups,)),
        ],
        compiler_params=pltpu.CompilerParams(
            collective_id=0, has_side_effects=True, vmem_limit_bytes=32 * 1024 * 1024
        ),
        cost_estimate=pl.CostEstimate(
            flops=300 * span * width, bytes_accessed=9 * span * width * 2, transcendentals=0
        ),
    )(
        *[
            pltpu.with_memory_space_constraint(operand, pltpu.HBM)
            for operand in (
                cotangent.reshape(block),
                level_input.reshape(block),
                saved_forward.reshape((top,) + block),
                saved_reverse.reshape((top,) + block),
                filters,
                by_level,
            )
        ]
    )
    results = (grad_input, grad_filters, grad_mixing)
    grad_input, grad_filters, grad_mixing = pl.pallas_call(
        hand_over,
        out_shape=tuple(pltpu.HBM(x.shape, x.dtype) for x in results),
        in_specs=[vmem] * 3,
        out_specs=(hbm,) * 3,
        scratch_shapes=[dma((3,))],
        cost_estimate=pl.CostEstimate(flops=0, bytes_accessed=2 * span * width * 2, transcendentals=0),
    )(*[pltpu.with_memory_space_constraint(x, pltpu.VMEM) for x in results])
    return (grad_input.reshape(level_input.shape), grad_filters, grad_mixing.transpose(1, 0, 2))


def solution(mesh):
    return jax.shard_map(
        body,
        mesh=mesh,
        in_specs=(
            P("dp", "ctx", None),
            P(None, "dp", "ctx", None),
            P(None, "dp", "ctx", None),
            P(),
            P(),
            P("dp", "ctx", None),
        ),
        out_specs=(P("dp", "ctx", None), P(), P()),
        check_vma=False,
    )
```
